256 devices in a mesh: rep: 64 (over x_lo, z, y), fsdp: 4 (over x_hi, core).
Axes of the slice: x: 4 (x_hi: 2, x_lo: 2; x = x_hi * 2 + x_lo), y: 4, z: 8, core: 2. Of those that a mesh axis runs over, the one named last changes fastest.
Arguments:
- weight: bfloat16 [64, 4096, 512], P('rep', 'fsdp'), may hold values from -6 to 6
- adam_first: bfloat16 [64, 4096, 512], P('rep', 'fsdp'), may hold values from -3.0517578e-05 to 3.0517578e-05
- adam_second: bfloat16 [64, 4096, 512], P('rep', 'fsdp'), may hold values from 4.7464255e-12 to 4.7521098e-11
- anchor: bfloat16 [4096, 512], P('fsdp'), may hold values from -6 to 6
- momentum: float32 [4096, 512], P('fsdp'), may hold values from -6 to 6
- tokens: bfloat16 [64, 1536, 4096], P('rep', 'fsdp'), may hold values from -20 to 20
- cotangent: bfloat16 [64, 1536, 512], P('rep', 'fsdp'), may hold values from -12 to 12
- plan: int32 [512], P('fsdp'), may hold values from 0 to 1
- mix_weights: float32 [4], replicated, may hold values from 0.2 to 0.8
- mix_index: int32 [64], P('rep'), may hold values from 0 to 3
Outputs:
- new_weight: bfloat16 [64, 4096, 512], P('rep', 'fsdp')
- new_momentum: float32 [4096, 512], P('fsdp')
The draws below stay inside these ranges and needn't reach their ends.
All inputs are finite; a program needn't handle non-finite values.
Results may differ from the reference program's by a relative error of at most 0.0054.
Values may be sent and summed in bfloat16 or wider, within the bound.
A program may use at most 128 MiB of HBM per device.

```python
import math
import jax
import jax.numpy as jnp
from jax import lax

D = 4096
HD = 128
C = 512
FRAG = 2
ROWS = 8
GROUPS = 512
MIXES = 4
TOK_DEV = 384
TOKENS = 1536
REPS = 64
N_FSDP = 4


def draw_tokens(key, part):
    key = jax.random.fold_in(key, 11)
    noise_key, scale_key = jax.random.split(key, 2)
    position = jnp.arange(D, dtype=jnp.float32) / D
    spread = jax.random.uniform(scale_key, (REPS, 1, D), jnp.float32, 0.0, 1.0)
    values = jnp.clip(jax.random.normal(noise_key, (REPS, TOKENS, D), jnp.float32), -4.0, 4.0)
    trend = 9.0 ** (0.5 * position)
    scale = 0.25 * 4.0 ** spread * trend[None, None, :]
    return (values * scale).astype(jnp.bfloat16)


def draw_cotangent(key, part):
    key = jax.random.fold_in(key, 23)
    noise_key, scale_key = jax.random.split(key, 2)
    spread = jax.random.uniform(scale_key, (REPS, 1, C), jnp.float32, 0.0, 1.0)
    values = jnp.clip(jax.random.normal(noise_key, (REPS, TOKENS, C), jnp.float32), -4.0, 4.0)
    scale = 0.3 * 10.0 ** spread
    return (values * scale).astype(jnp.bfloat16)


def touch_ends(values, rng, low, high):
    longest = values.shape.index(max(values.shape))
    spots = []
    for shift in (0, 1):
        where = [jax.random.randint(jax.random.fold_in(rng, axis), (), 0, length) for axis, length in enumerate(values.shape)]
        where[longest] = (where[longest] + shift) % values.shape[longest]
        spots.append(tuple(where))
    return values.at[spots[0]].set(low).at[spots[1]].set(high)


def level_of(own_key, extent, cuts, least, top_value):
    loudness, own = 1.0, jax.random.fold_in(own_key, 6)
    for axis_at, blocks in cuts:
        steps = jnp.exp(jax.random.uniform(jax.random.fold_in(own, axis_at), (blocks,), jnp.float32, least / len(cuts), top_value / len(cuts)))
        loudness = loudness * jnp.repeat(steps, extent[axis_at] // blocks).reshape([-1 if axis == axis_at else 1 for axis in range(len(extent))])
    return loudness


def scatter_about(key, dims, width, limit, shards=(), kind=jnp.bfloat16):
    loudness = level_of(key, dims, shards, -0.22, 0.18) if shards else 1.0
    entries = jax.random.normal(key, dims, jnp.float32) * width * loudness
    return jnp.minimum(jnp.maximum(entries, -limit), limit).astype(kind)


def setup_inputs(seed: int = 0) -> dict:
    splits = jax.random.split(jax.random.key(seed), 11)
    return {
        "weight": scatter_about(splits[0], (REPS, D, C), 1.0, 6.0, ((0, 64), (1, 4))),
        "adam_first": scatter_about(splits[1], (REPS, D, C), (0.003 * (D * C) ** -0.5), 3.0517578125e-05, ((0, 64), (1, 4))),
        "adam_second": jnp.clip(jnp.exp(math.log(4.75210981676355e-11) - 2.303782 * jax.random.uniform(splits[2], (REPS, D, C), jnp.float32) ** level_of(splits[2], (REPS, D, C), ((0, 64), (1, 4)), -0.2, 0.2)), 4.746425474877469e-12, 4.75210981676355e-11).astype(jnp.bfloat16),
        "anchor": scatter_about(splits[3], (D, C), 1.0, 6.0, ((0, 4),)),
        "momentum": scatter_about(splits[4], (D, C), 0.5, 6.0, ((0, 4),), jnp.float32),
        "tokens": draw_tokens(jax.random.fold_in(splits[10], 71), 0),
        "cotangent": draw_cotangent(jax.random.fold_in(splits[10], 71), 0),
        "plan": touch_ends(jax.random.randint(splits[7], (GROUPS,), 0, FRAG), jax.random.fold_in(splits[7], 1), 0, FRAG - 1).astype(jnp.int32),
        "mix_weights": jnp.clip(jax.random.uniform(splits[8], (MIXES,), jnp.float32, 0.2, 0.8), 0.2, 0.8),
        "mix_index": touch_ends(jax.random.randint(splits[9], (REPS,), 0, MIXES), jax.random.fold_in(splits[9], 1), 0, MIXES - 1).astype(jnp.int32),
    }


EPS_NORM = 1e-06
BETA_ONE = 0.9
BETA_TWO = 0.999
ADAM_EPS = 1e-08
LEARN_RATE = 0.3
DECAY = 0.1
CLIP = 0.05
MOMENT_COEF = 0.9
OUTER_RATE = 0.7

def head_norm(keys):
    heads = keys.reshape(keys.shape[0], -1, HD)
    factor = lax.rsqrt(lax.optimization_barrier(jnp.mean(heads * heads, axis=-1, keepdims=True)) + EPS_NORM)
    return (heads * factor).reshape(keys.shape)

def key_cotangent(keys, cot):
    _, pullback = jax.vjp(head_norm, keys)
    return pullback(cot.astype(jnp.float32))[0].astype(jnp.bfloat16)

def inner_step(operands):
    weight_r, first_r, second_r, inputs, cot = operands
    keys = jnp.dot(inputs, weight_r, preferred_element_type=jnp.float32)
    dkeys = key_cotangent(keys, cot)
    blocks_x = inputs.reshape(N_FSDP, TOK_DEV, D).astype(jnp.float32)
    blocks_d = dkeys.reshape(N_FSDP, TOK_DEV, C).astype(jnp.float32)
    parts = jnp.einsum('ntd,ntc->ndc', blocks_x, blocks_d).astype(jnp.bfloat16)
    grad = lax.optimization_barrier(jnp.sum(parts.astype(jnp.float32), axis=0)) / TOKENS
    total = jnp.sqrt(jnp.sum(grad * grad) + 1e-12)
    clipped = grad * jnp.minimum(1.0, CLIP / total)
    first = BETA_ONE * first_r.astype(jnp.float32) + (1.0 - BETA_ONE) * clipped
    second = BETA_TWO * second_r.astype(jnp.float32) + (1.0 - BETA_TWO) * clipped * clipped
    wide = weight_r.astype(jnp.float32)
    return wide - LEARN_RATE * (first / (jnp.sqrt(second) + ADAM_EPS) + DECAY * wide)

def reference(weight, adam_first, adam_second, anchor, momentum, tokens, cotangent, plan, mix_weights, mix_index):
    inner = lax.map(inner_step, (weight, adam_first, adam_second, tokens, cotangent))
    alpha = mix_weights[mix_index]
    columns = jnp.arange(C, dtype=jnp.int32) // (C // FRAG)
    row_frag = plan[jnp.arange(D, dtype=jnp.int32) // ROWS]
    chosen = columns[None, :] == row_frag[:, None]
    base = anchor.astype(jnp.float32)
    summed = lax.fori_loop(0, REPS, lambda r, acc: acc + (base - weight[r].astype(jnp.float32)), jnp.zeros((D, C), jnp.float32))
    average = summed / REPS
    moved = MOMENT_COEF * momentum + average
    new_momentum = jnp.where(chosen, moved, momentum)
    outer = base - OUTER_RATE * (average + MOMENT_COEF * moved)
    blended = alpha[:, None, None] * inner + (1.0 - alpha[:, None, None]) * outer[None]
    new_weight = jnp.where(chosen[None], blended, inner).astype(jnp.bfloat16)
    return (new_weight, new_momentum)
```

```python
import functools

import jax
import jax.numpy as jnp
from jax import lax
from jax.experimental import pallas as pl
from jax.experimental.pallas import tpu as pltpu
from jax.sharding import PartitionSpec as P

HD = 128
ROWS = 8
EPS_NORM = 1e-06
BETA_ONE = 0.9
BETA_TWO = 0.999
ADAM_EPS = 1e-08
LEARN_RATE = 0.3
DECAY = 0.1
CLIP = 0.05
MOMENT_COEF = 0.9
OUTER_RATE = 0.7

MESH = pl.DeviceIdType.MESH
F32 = jnp.float32
BF16 = jnp.bfloat16

NY = 4
NZ = 8
REPS = 64
TOK = 384
FEAT = 1024
COLS = 512
HALF = 256
PARTS = 4
PROWS = FEAT // PARTS
YROWS = FEAT // NY
ZROWS = YROWS // NZ


def place(x_lo, z, y, f):
    return (x_lo * (NZ * NY) + z * NY + y, f)


def kernel(
    weight,
    adam_first,
    adam_second,
    anchor,
    momentum,
    tokens,
    cotangent,
    plan,
    mix_weights,
    mix_index,
    new_weight,
    new_momentum,
    wown,
    wrecv,
    tch,
    tt,
    cot,
    mask,
    picked,
    yrecv,
    ysum,
    zrecv,
    zsum,
    xrecv,
    mean,
    psend,
    precv,
    dch,
    gsend,
    grecv,
    gown,
    first,
    second,
    base,
    old,
    level,
    factor,
    sq,
    load_sem,
    wsend_sem,
    wrecv_sem,
    tsend_sem,
    trecv_sem,
    ysend_sem,
    yrecv_sem,
    zsend_sem,
    zrecv_sem,
    xsend_sem,
    xrecv_sem,
    azsend_sem,
    azrecv_sem,
    aysend_sem,
    ayrecv_sem,
    psend_sem,
    precv_sem,
    dsend_sem,
    drecv_sem,
    gsend_sem,
    grecv_sem,
    qsend_sem,
    qrecv_sem,
):
    rep = lax.axis_index("rep")
    f = lax.axis_index("fsdp")
    x_lo = rep // (NZ * NY)
    z = (rep // NY) % NZ
    y = rep % NY
    mate_f = f + 1 - 2 * (f % 2)
    across_f = (f + 2) % 4
    diag_f = 3 - f
    mate = (rep, mate_f)
    across = (rep, across_f)
    diag = (rep, diag_f)
    y_peers = [place(x_lo, z, (y + d) % NY, f) for d in range(1, NY)]
    z_peers = [place(x_lo, (z + d) % NZ, y, f) for d in range(1, NZ)]
    x_peer = place(1 - x_lo, z, y, f)

    barrier = pltpu.get_barrier_semaphore()
    peers = [across, mate, diag, x_peer] + y_peers + z_peers
    for peer in peers:
        pl.semaphore_signal(barrier, inc=1, device_id=peer, device_id_type=MESH)

    def columns(index):
        return pl.ds(pl.multiple_of(index * FEAT, FEAT), FEAT)

    loads = [
        pltpu.make_async_copy(weight.at[0], wown, load_sem.at[0]),
        pltpu.make_async_copy(
            tokens.at[0, :, columns(f)], tch.at[0, :, pl.ds(0, FEAT)], load_sem.at[1]
        ),
        pltpu.make_async_copy(
            tokens.at[0, :, columns(across_f)], tch.at[0, :, pl.ds(FEAT, FEAT)], load_sem.at[2]
        ),
        pltpu.make_async_copy(cotangent.at[0], cot, load_sem.at[3]),
        pltpu.make_async_copy(anchor, base, load_sem.at[4]),
        pltpu.make_async_copy(momentum, old, load_sem.at[5]),
        pltpu.make_async_copy(adam_first.at[0], first, load_sem.at[6]),
        pltpu.make_async_copy(adam_second.at[0], second, load_sem.at[7]),
    ]
    for copy in loads:
        copy.start()

    def mark(i, _):
        mask[pl.ds(pl.multiple_of(i * ROWS, ROWS), ROWS), :] = jnp.full((ROWS, HD), plan[i], jnp.int32)
        return 0

    lax.fori_loop(0, FEAT // ROWS, mark, 0, unroll=8)

    pl.semaphore_wait(barrier, len(peers))

    def remote(src, dst, send, recv, to):
        return pltpu.make_async_remote_copy(
            src_ref=src, dst_ref=dst, send_sem=send, recv_sem=recv, device_id=to, device_id_type=MESH
        )

    w_copies = [
        remote(
            weight.at[0, :, pl.ds(j * HALF, HALF)], wrecv.at[j], wsend_sem.at[j], wrecv_sem.at[j], across
        )
        for j in range(2)
    ]
    for copy in w_copies:
        copy.start()
    t_copies = [
        remote(
            tokens.at[0, :, columns(index)],
            tch.at[1, :, pl.ds(b * FEAT, FEAT)],
            tsend_sem.at[b],
            trecv_sem.at[b],
            mate,
        )
        for b, index in enumerate((mate_f, diag_f))
    ]
    for copy in t_copies:
        copy.start()

    loads[0].wait()

    def pick(start):
        def body(i, _):
            rows = pl.ds(pl.multiple_of(start + i * 32, 32), 32)
            chosen = mask[rows, :] == 0
            for k in range(HALF // HD):
                low = wown[rows, k * HD : (k + 1) * HD].astype(F32)
                high = wown[rows, HALF + k * HD : HALF + (k + 1) * HD].astype(F32)
                picked[rows, k * HD : (k + 1) * HD] = jnp.where(chosen, low, high).astype(BF16)
            return 0

        lax.fori_loop(0, YROWS // 32, body, 0, unroll=2)

    y_copies = []
    for d in range(1, NY):
        start = ((y + d) % NY) * YROWS
        pick(start)
        y_copies.append(
            remote(
                picked.at[pl.ds(pl.multiple_of(start, YROWS), YROWS)],
                yrecv.at[d - 1],
                ysend_sem.at[d - 1],
                yrecv_sem.at[d - 1],
                y_peers[d - 1],
            )
        )
        y_copies[-1].start()
    pick(y * YROWS)

    def turn(t):
        def body(i, _):
            at = pl.multiple_of(i * HD, HD)
            tt[pl.ds(at, HD), t * TOK : (t + 1) * TOK] = tch[t, :, pl.ds(at, HD)].T
            return 0

        lax.fori_loop(0, 2 * FEAT // HD, body, 0)

    loads[1].wait()
    loads[2].wait()
    turn(0)

    for copy in y_copies:
        copy.wait_recv()

    def add_y(i, _):
        at = pl.multiple_of(i * 32, 32)
        rows = pl.ds(at, 32)
        total = picked[pl.ds(pl.multiple_of(y * YROWS + i * 32, 32), 32), :].astype(F32)
        for d in range(NY - 1):
            total = total + yrecv[d, rows, :].astype(F32)
        ysum[rows, :] = total
        return 0

    lax.fori_loop(0, YROWS // 32, add_y, 0)
    z_copies = []
    for d in range(1, NZ):
        start = pl.multiple_of(((z + d) % NZ) * ZROWS, ZROWS)
        z_copies.append(
            remote(
                ysum.at[pl.ds(start, ZROWS)],
                zrecv.at[d - 1],
                zsend_sem.at[d - 1],
                zrecv_sem.at[d - 1],
                z_peers[d - 1],
            )
        )
        z_copies[-1].start()

    for copy in t_copies:
        copy.wait_recv()
    turn(1)
    loads[3].wait()

    own_block = pl.ds(0, FEAT)
    across_block = pl.ds(FEAT, FEAT)
    p_copies = []
    d_copies = []
    g_copies = []

    def project(t, j):
        mine = jnp.dot(
            tch[t, :, own_block], wown[:, j * HALF : (j + 1) * HALF], preferred_element_type=F32
        )
        return mine + jnp.dot(tch[t, :, across_block], wrecv[j], preferred_element_type=F32)

    def chunk(j):
        w_copies[j].wait_recv()
        psend[j] = project(1, j)
        p_copy = remote(psend.at[j], precv.at[j], psend_sem.at[j], precv_sem.at[j], mate)
        p_copy.start()
        p_copies.append(p_copy)
        keys = project(0, j)
        p_copy.wait_recv()
        keys = keys + precv[j]
        for k in range(HALF // HD):
            at = j * HALF + k * HD
            head = keys[:, k * HD : (k + 1) * HD]
            pull = cot[:, at : at + HD].astype(F32)
            scale = lax.rsqrt(jnp.sum(head * head, axis=1, keepdims=True) * (1.0 / HD) + EPS_NORM)
            inner = jnp.sum(head * pull, axis=1, keepdims=True) * (1.0 / HD)
            back = scale * (pull - head * (scale * scale * inner))
            dch[j, 0, :, k * HD : (k + 1) * HD] = back.astype(BF16)
        d_copy = remote(dch.at[j, 0], dch.at[j, 1], dsend_sem.at[j], drecv_sem.at[j], mate)
        d_copy.start()
        d_copies.append(d_copy)
        d_copy.wait_recv()

        def grad(at):
            low = jnp.dot(tt[pl.ds(at, PROWS), 0:TOK], dch[j, 0], preferred_element_type=F32)
            high = jnp.dot(
                tt[pl.ds(at, PROWS), TOK : 2 * TOK], dch[j, 1], preferred_element_type=F32
            )
            return low + high

        for i in range(PARTS):
            gsend[j, i] = grad(FEAT + i * PROWS).astype(BF16)
            g_copy = remote(
                gsend.at[j, i], grecv.at[j, i], gsend_sem.at[j, i], grecv_sem.at[j, i], across
            )
            g_copy.start()
            g_copies.append(g_copy)
        for i in range(PARTS):
            gown[j, i] = grad(i * PROWS)

    chunk(0)

    for copy in z_copies:
        copy.wait_recv()
    total = ysum[pl.ds(pl.multiple_of(z * ZROWS, ZROWS), ZROWS), :]
    for d in range(NZ - 1):
        total = total + zrecv[d]
    zsum[...] = total
    x_copy = remote(zsum, xrecv, xsend_sem, xrecv_sem, x_peer)
    x_copy.start()
    x_copy.wait_recv()
    mine = pl.ds(pl.multiple_of(y * YROWS + z * ZROWS, ZROWS), ZROWS)
    mean[mine, :] = (zsum[...] + xrecv[...]) * (1.0 / REPS)
    az_copies = []
    for d in range(1, NZ):
        az_copies.append(
            remote(
                mean.at[mine], mean.at[mine], azsend_sem.at[d - 1], azrecv_sem.at[d - 1], z_peers[d - 1]
            )
        )
        az_copies[-1].start()

    chunk(1)

    for copy in az_copies:
        copy.wait_recv()
    block = pl.ds(pl.multiple_of(y * YROWS, YROWS), YROWS)
    ay_copies = []
    for d in range(1, NY):
        ay_copies.append(
            remote(
                mean.at[block],
                mean.at[block],
                aysend_sem.at[d - 1],
                ayrecv_sem.at[d - 1],
                y_peers[d - 1],
            )
        )
        ay_copies[-1].start()

    def gather(j, i, total):
        g_copies[j * PARTS + i].wait_recv()

        def body(s, total):
            rows = pl.ds(pl.multiple_of(s * 32, 32), 32)
            grad = (gown[j, i, rows, :] + grecv[j, i, rows, :].astype(F32)) * (1.0 / (4 * TOK))
            gown[j, i, rows, :] = grad
            square = grad * grad
            for r in range(4):
                for k in range(HALF // HD):
                    total = total + square[r * 8 : (r + 1) * 8, k * HD : (k + 1) * HD]
            return total

        return lax.fori_loop(0, PROWS // 32, body, total, unroll=2)

    squares = jnp.zeros((8, HD), F32)
    for i in range(PARTS):
        squares = gather(0, i, squares)

    for copy in loads[4:]:
        copy.wait()
    choice = mix_index[0]
    alpha = mix_weights[0]
    for k in range(1, 4):
        alpha = jnp.where(choice == k, mix_weights[k], alpha)
    for copy in ay_copies:
        copy.wait_recv()

    def outer_step(i, _):
        rows = pl.ds(pl.multiple_of(i * 16, 16), 16)
        row_frag = mask[rows, :]
        for k in range(HALF // HD):
            middle = mean[rows, k * HD : (k + 1) * HD]
            for index in range(2):
                at = index * HALF + k * HD
                chosen = row_frag == index
                start = base[rows, at : at + HD].astype(F32)
                wide = wown[rows, at : at + HD].astype(F32) * (1.0 - LEARN_RATE * DECAY)
                before = old[rows, at : at + HD]
                average = start - middle
                moved = MOMENT_COEF * before + average
                outer = start - OUTER_RATE * (average + MOMENT_COEF * moved)
                new_momentum[rows, at : at + HD] = jnp.where(chosen, moved, before)
                level[rows, at : at + HD] = jnp.where(
                    chosen, alpha * wide + (1.0 - alpha) * outer, wide
                )
        return 0

    lax.fori_loop(0, FEAT // 16, outer_step, 0)

    for i in range(PARTS):
        squares = gather(1, i, squares)
    sq[0] = squares
    q_copies = []
    for d, peer in enumerate((mate, across, diag)):
        q_copies.append(remote(sq.at[0], sq.at[1 + d], qsend_sem.at[d], qrecv_sem.at[d], peer))
        q_copies[-1].start()
    for copy in q_copies:
        copy.wait_recv()
    everything = jnp.sum(sq[0] + sq[1] + sq[2] + sq[3], keepdims=True)
    clip = jnp.minimum(1.0, CLIP / jnp.sqrt(everything + 1e-12))
    factor[...] = jnp.broadcast_to(clip, (8, HD))

    for j in range(2):
        for i in range(PARTS):

            def adam(s, _, j=j, i=i):
                at = pl.multiple_of(s * 16, 16)
                rows = pl.ds(pl.multiple_of(i * PROWS + s * 16, 16), 16)
                ratio = jnp.concatenate([factor[...]] * 2, axis=0)
                chosen_row = mask[rows, :]
                rate = jnp.where(chosen_row == j, alpha * LEARN_RATE, LEARN_RATE)
                for k in range(HALF // HD):
                    c = j * HALF + k * HD
                    clipped = gown[j, i, pl.ds(at, 16), k * HD : (k + 1) * HD] * ratio
                    one = BETA_ONE * first[rows, c : c + HD].astype(F32) + (1.0 - BETA_ONE) * clipped
                    two = (
                        BETA_TWO * second[rows, c : c + HD].astype(F32)
                        + (1.0 - BETA_TWO) * clipped * clipped
                    )
                    step = one / (jnp.sqrt(two) + ADAM_EPS)
                    new_weight[0, rows, c : c + HD] = (
                        level[rows, c : c + HD] - rate * step
                    ).astype(BF16)
                return 0

            lax.fori_loop(0, PROWS // 16, adam, 0, unroll=4)

    sent = w_copies + t_copies + y_copies + z_copies + [x_copy] + az_copies + ay_copies
    for copy in sent + p_copies + d_copies + g_copies + q_copies:
        copy.wait_send()


def local(*args):
    dma = pltpu.SemaphoreType.DMA
    any_space = pl.BlockSpec(memory_space=pl.ANY)
    smem = pl.BlockSpec(memory_space=pltpu.SMEM)
    vmem = pl.BlockSpec(memory_space=pltpu.VMEM)
    return pl.pallas_call(
        kernel,
        name="diloco_step",
        out_shape=(
            jax.ShapeDtypeStruct((1, FEAT, COLS), BF16),
            jax.ShapeDtypeStruct((FEAT, COLS), F32),
        ),
        in_specs=[any_space] * 7 + [smem] * 3,
        out_specs=(vmem, vmem),
        scratch_shapes=[
            pltpu.VMEM((FEAT, COLS), BF16),
            pltpu.VMEM((2, FEAT, HALF), BF16),
            pltpu.VMEM((2, TOK, 2 * FEAT), BF16),
            pltpu.VMEM((2 * FEAT, 2 * TOK), BF16),
            pltpu.VMEM((TOK, COLS), BF16),
            pltpu.VMEM((FEAT, HD), jnp.int32),
            pltpu.VMEM((FEAT, HALF), BF16),
            pltpu.VMEM((NY - 1, YROWS, HALF), BF16),
            pltpu.VMEM((YROWS, HALF), F32),
            pltpu.VMEM((NZ - 1, ZROWS, HALF), F32),
            pltpu.VMEM((ZROWS, HALF), F32),
            pltpu.VMEM((ZROWS, HALF), F32),
            pltpu.VMEM((FEAT, HALF), F32),
            pltpu.VMEM((2, TOK, HALF), F32),
            pltpu.VMEM((2, TOK, HALF), F32),
            pltpu.VMEM((2, 2, TOK, HALF), BF16),
            pltpu.VMEM((2, PARTS, PROWS, HALF), BF16),
            pltpu.VMEM((2, PARTS, PROWS, HALF), BF16),
            pltpu.VMEM((2, PARTS, PROWS, HALF), F32),
            pltpu.VMEM((FEAT, COLS), BF16),
            pltpu.VMEM((FEAT, COLS), BF16),
            pltpu.VMEM((FEAT, COLS), BF16),
            pltpu.VMEM((FEAT, COLS), F32),
            pltpu.VMEM((FEAT, COLS), F32),
            pltpu.VMEM((8, HD), F32),
            pltpu.VMEM((4, 8, HD), F32),
            dma((8,)),
            dma((2,)),
            dma((2,)),
            dma((2,)),
            dma((2,)),
            dma((NY - 1,)),
            dma((NY - 1,)),
            dma((NZ - 1,)),
            dma((NZ - 1,)),
            dma,
            dma,
            dma((NZ - 1,)),
            dma((NZ - 1,)),
            dma((NY - 1,)),
            dma((NY - 1,)),
            dma((2,)),
            dma((2,)),
            dma((2,)),
            dma((2,)),
            dma((2, PARTS)),
            dma((2, PARTS)),
            dma((3,)),
            dma((3,)),
        ],
        compiler_params=pltpu.CompilerParams(
            collective_id=0, has_side_effects=True, vmem_limit_bytes=40 * 2**20
        ),
    )(*args)


def solution(mesh):
    placed = (
        P("rep", "fsdp", None),
        P("rep", "fsdp", None),
        P("rep", "fsdp", None),
        P("fsdp", None),
        P("fsdp", None),
        P("rep", "fsdp", None),
        P("rep", "fsdp", None),
        P("fsdp"),
        P(),
        P("rep"),
    )
    return jax.shard_map(
        local,
        mesh=mesh,
        in_specs=placed,
        out_specs=(P("rep", "fsdp", None), P("fsdp", None)),
        check_vma=False,
    )
```

```python
import functools

import jax
import jax.numpy as jnp
from jax import lax
from jax.experimental import pallas as pl
from jax.experimental.pallas import tpu as pltpu
from jax.sharding import PartitionSpec as P

HD = 128
ROWS = 8
EPS_NORM = 1e-06
BETA_ONE = 0.9
BETA_TWO = 0.999
ADAM_EPS = 1e-08
LEARN_RATE = 0.3
DECAY = 0.1
CLIP = 0.05
MOMENT_COEF = 0.9
OUTER_RATE = 0.7

MESH = pl.DeviceIdType.MESH
F32 = jnp.float32
BF16 = jnp.bfloat16

NY = 4
NZ = 8
REPS = 64
TOK = 384
FEAT = 1024
COLS = 512
HALF = 256
PARTS = 4
PROWS = FEAT // PARTS
YROWS = FEAT // NY
ZROWS = YROWS // NZ
NEAR = (1, 7, 2, 6, 3, 5, 4)


def place(x_lo, z, y, f):
    return (x_lo * (NZ * NY) + z * NY + y, f)


def kernel(
    weight,
    adam_first,
    adam_second,
    anchor,
    momentum,
    tokens,
    cotangent,
    plan_in,
    mix_weights_in,
    mix_index,
    new_weight,
    new_momentum,
    plan,
    mix_weights,
    wown,
    wrecv,
    tch,
    tt,
    begun,
    cot,
    mask,
    picked,
    yrecv,
    ysum,
    zrecv,
    zsum,
    xrecv,
    mean,
    psend,
    precv,
    dch,
    gsend,
    grecv,
    gown,
    first,
    second,
    base,
    old,
    level,
    factor,
    sq,
    small_sem,
    load_sem,
    wsend_sem,
    wrecv_sem,
    tsend_sem,
    trecv_sem,
    ysend_sem,
    yrecv_sem,
    zsend_sem,
    zrecv_sem,
    xsend_sem,
    xrecv_sem,
    azsend_sem,
    azrecv_sem,
    aysend_sem,
    ayrecv_sem,
    psend_sem,
    precv_sem,
    dsend_sem,
    drecv_sem,
    gsend_sem,
    grecv_sem,
    qsend_sem,
    qrecv_sem,
):
    rep = lax.axis_index("rep")
    f = lax.axis_index("fsdp")
    x_lo = rep // (NZ * NY)
    z = (rep // NY) % NZ
    y = rep % NY
    mate_f = f + 1 - 2 * (f % 2)
    across_f = (f + 2) % 4
    diag_f = 3 - f
    mate = (rep, mate_f)
    across = (rep, across_f)
    diag = (rep, diag_f)
    y_peers = [place(x_lo, z, (y + d) % NY, f) for d in range(1, NY)]
    z_peers = [place(x_lo, (z + d) % NZ, y, f) for d in range(1, NZ)]
    x_peer = place(1 - x_lo, z, y, f)

    barrier = pltpu.get_barrier_semaphore()
    peers = [across, mate, diag, x_peer] + y_peers + z_peers
    for peer in peers:
        pl.semaphore_signal(barrier, inc=1, device_id=peer, device_id_type=MESH)

    def columns(index):
        return pl.ds(pl.multiple_of(index * FEAT, FEAT), FEAT)

    small = [
        pltpu.make_async_copy(plan_in, plan, small_sem.at[0]),
        pltpu.make_async_copy(mix_weights_in, mix_weights, small_sem.at[1]),
    ]
    for copy in small:
        copy.start()
    loads = [
        pltpu.make_async_copy(weight.at[0], wown, load_sem.at[0]),
        pltpu.make_async_copy(
            tokens.at[0, :, columns(f)], tch.at[0, :, pl.ds(0, FEAT)], load_sem.at[1]
        ),
        pltpu.make_async_copy(
            tokens.at[0, :, columns(across_f)], tch.at[0, :, pl.ds(FEAT, FEAT)], load_sem.at[2]
        ),
        pltpu.make_async_copy(cotangent.at[0], cot, load_sem.at[3]),
        pltpu.make_async_copy(anchor, base, load_sem.at[4]),
        pltpu.make_async_copy(momentum, old, load_sem.at[5]),
        pltpu.make_async_copy(adam_first.at[0], first, load_sem.at[6]),
        pltpu.make_async_copy(adam_second.at[0], second, load_sem.at[7]),
    ]
    for copy in loads:
        copy.start()

    for copy in small:
        copy.wait()

    def mark(i, _):
        mask[pl.ds(pl.multiple_of(i * ROWS, ROWS), ROWS), :] = jnp.full((ROWS, HD), plan[i], jnp.int32)
        return 0

    lax.fori_loop(0, FEAT // ROWS, mark, 0, unroll=8)

    pl.semaphore_wait(barrier, len(peers))

    def remote(src, dst, send, recv, to):
        return pltpu.make_async_remote_copy(
            src_ref=src, dst_ref=dst, send_sem=send, recv_sem=recv, device_id=to, device_id_type=MESH
        )

    w_copies = [
        remote(
            weight.at[0, :, pl.ds(j * HALF, HALF)], wrecv.at[j], wsend_sem.at[j], wrecv_sem.at[j], across
        )
        for j in range(2)
    ]
    for copy in w_copies:
        copy.start()
    t_copies = [
        remote(
            tokens.at[0, :, columns(index)],
            tch.at[1, :, pl.ds(b * FEAT, FEAT)],
            tsend_sem.at[b],
            trecv_sem.at[b],
            mate,
        )
        for b, index in enumerate((mate_f, diag_f))
    ]
    for copy in t_copies:
        copy.start()

    loads[0].wait()

    def pick(start):
        def body(i, _):
            rows = pl.ds(pl.multiple_of(start + i * 32, 32), 32)
            chosen = mask[rows, :] == 0
            for k in range(HALF // HD):
                low = wown[rows, k * HD : (k + 1) * HD].astype(F32)
                high = wown[rows, HALF + k * HD : HALF + (k + 1) * HD].astype(F32)
                picked[rows, k * HD : (k + 1) * HD] = jnp.where(chosen, low, high).astype(BF16)
            return 0

        lax.fori_loop(0, YROWS // 32, body, 0, unroll=2)

    y_copies = []
    for d in range(1, NY):
        start = ((y + d) % NY) * YROWS
        pick(start)
        y_copies.append(
            remote(
                picked.at[pl.ds(pl.multiple_of(start, YROWS), YROWS)],
                yrecv.at[d - 1],
                ysend_sem.at[d - 1],
                yrecv_sem.at[d - 1],
                y_peers[d - 1],
            )
        )
        y_copies[-1].start()
    pick(y * YROWS)

    def turn(t):
        def body(i, _):
            at = pl.multiple_of(i * HD, HD)
            tt[pl.ds(at, HD), t * TOK : (t + 1) * TOK] = tch[t, :, pl.ds(at, HD)].T
            return 0

        lax.fori_loop(0, 2 * FEAT // HD, body, 0)

    loads[1].wait()
    loads[2].wait()
    turn(0)

    for copy in y_copies:
        copy.wait_recv()

    def add_y(i, _):
        at = pl.multiple_of(i * 32, 32)
        rows = pl.ds(at, 32)
        total = picked[pl.ds(pl.multiple_of(y * YROWS + i * 32, 32), 32), :].astype(F32)
        for d in range(NY - 1):
            total = total + yrecv[d, rows, :].astype(F32)
        ysum[rows, :] = total
        return 0

    lax.fori_loop(0, YROWS // 32, add_y, 0)
    z_copies = []
    for d in range(1, NZ):
        start = pl.multiple_of(((z + d) % NZ) * ZROWS, ZROWS)
        z_copies.append(
            remote(
                ysum.at[pl.ds(start, ZROWS)],
                zrecv.at[d - 1],
                zsend_sem.at[d - 1],
                zrecv_sem.at[d - 1],
                z_peers[d - 1],
            )
        )
        z_copies[-1].start()

    for copy in t_copies:
        copy.wait_recv()
    turn(1)
    loads[3].wait()

    own_block = pl.ds(0, FEAT)
    across_block = pl.ds(FEAT, FEAT)
    p_copies = []
    d_copies = []
    g_copies = []

    def prepare(t, j):
        begun[t, j] = jnp.dot(
            tch[t, :, own_block], wown[:, j * HALF : (j + 1) * HALF], preferred_element_type=F32
        )

    def project(t, j):
        return begun[t, j] + jnp.dot(tch[t, :, across_block], wrecv[j], preferred_element_type=F32)

    def add_z():
        for copy in z_copies:
            copy.wait_recv()
        total = ysum[pl.ds(pl.multiple_of(z * ZROWS, ZROWS), ZROWS), :]
        for d in range(NZ - 1):
            total = total + zrecv[d]
        zsum[...] = total
        x_copy.start()

    def slice_of(d):
        start = y * YROWS + ((z + NZ - d) % NZ) * ZROWS
        return pl.ds(pl.multiple_of(start, ZROWS), ZROWS)

    def spread(d):
        rows = slice_of(d)
        for e in range(NY - 1):
            copy = remote(
                mean.at[rows], mean.at[rows], aysend_sem.at[d, e], ayrecv_sem.at[d, e], y_peers[e]
            )
            copy.start()
            ay_copies.append(copy)

    def add_x():
        x_copy.wait_recv()
        rows = slice_of(0)
        mean[rows, :] = (zsum[...] + xrecv[...]) * (1.0 / REPS)
        for d in NEAR:
            az_copies[d] = remote(
                mean.at[rows], mean.at[rows], azsend_sem.at[d - 1], azrecv_sem.at[d - 1], z_peers[d - 1]
            )
            az_copies[d].start()
        spread(0)

    def forward(*steps):
        for d in steps:
            az_copies[d].wait_recv()
            spread(d)

    x_copy = remote(zsum, xrecv, xsend_sem, xrecv_sem, x_peer)
    az_copies = {}
    ay_copies = []

    def chunk(j):
        w_copies[j].wait_recv()
        psend[j] = project(1, j)
        p_copy = remote(psend.at[j], precv.at[j], psend_sem.at[j], precv_sem.at[j], mate)
        p_copy.start()
        p_copies.append(p_copy)
        keys = project(0, j)
        p_copy.wait_recv()
        keys = keys + precv[j]
        for k in range(HALF // HD):
            at = j * HALF + k * HD
            head = keys[:, k * HD : (k + 1) * HD]
            pull = cot[:, at : at + HD].astype(F32)
            scale = lax.rsqrt(jnp.sum(head * head, axis=1, keepdims=True) * (1.0 / HD) + EPS_NORM)
            inner = jnp.sum(head * pull, axis=1, keepdims=True) * (1.0 / HD)
            back = scale * (pull - head * (scale * scale * inner))
            dch[j, 0, :, k * HD : (k + 1) * HD] = back.astype(BF16)
        d_copy = remote(dch.at[j, 0], dch.at[j, 1], dsend_sem.at[j], drecv_sem.at[j], mate)
        d_copy.start()
        d_copies.append(d_copy)
        if j == 0:
            add_z()
        d_copy.wait_recv()

        def grad(at):
            low = jnp.dot(tt[pl.ds(at, PROWS), 0:TOK], dch[j, 0], preferred_element_type=F32)
            high = jnp.dot(
                tt[pl.ds(at, PROWS), TOK : 2 * TOK], dch[j, 1], preferred_element_type=F32
            )
            return low + high

        for i in range(PARTS):
            gsend[j, i] = grad(FEAT + i * PROWS).astype(BF16)
            g_copy = remote(
                gsend.at[j, i], grecv.at[j, i], gsend_sem.at[j, i], grecv_sem.at[j, i], across
            )
            g_copy.start()
            g_copies.append(g_copy)
        for i in range(PARTS):
            gown[j, i] = grad(i * PROWS)

    for t in range(2):
        for j in range(2):
            prepare(t, j)

    chunk(0)
    add_x()
    chunk(1)
    forward(*NEAR)

    def gather(j, i, total):
        g_copies[j * PARTS + i].wait_recv()

        def body(s, total):
            rows = pl.ds(pl.multiple_of(s * 32, 32), 32)
            grad = (gown[j, i, rows, :] + grecv[j, i, rows, :].astype(F32)) * (1.0 / (4 * TOK))
            gown[j, i, rows, :] = grad
            square = grad * grad
            for r in range(4):
                for k in range(HALF // HD):
                    total = total + square[r * 8 : (r + 1) * 8, k * HD : (k + 1) * HD]
            return total

        return lax.fori_loop(0, PROWS // 32, body, total, unroll=2)

    squares = jnp.zeros((8, HD), F32)
    for i in range(PARTS):
        squares = gather(0, i, squares)

    for copy in loads[4:]:
        copy.wait()
    choice = mix_index[0]
    alpha = mix_weights[0]
    for k in range(1, 4):
        alpha = jnp.where(choice == k, mix_weights[k], alpha)
    for copy in ay_copies:
        copy.wait_recv()

    def outer_step(i, _):
        rows = pl.ds(pl.multiple_of(i * 16, 16), 16)
        row_frag = mask[rows, :]
        for k in range(HALF // HD):
            middle = mean[rows, k * HD : (k + 1) * HD]
            for index in range(2):
                at = index * HALF + k * HD
                chosen = row_frag == index
                start = base[rows, at : at + HD].astype(F32)
                wide = wown[rows, at : at + HD].astype(F32) * (1.0 - LEARN_RATE * DECAY)
                before = old[rows, at : at + HD]
                average = start - middle
                moved = MOMENT_COEF * before + average
                outer = start - OUTER_RATE * (average + MOMENT_COEF * moved)
                new_momentum[rows, at : at + HD] = jnp.where(chosen, moved, before)
                level[rows, at : at + HD] = jnp.where(
                    chosen, alpha * wide + (1.0 - alpha) * outer, wide
                )
        return 0

    lax.fori_loop(0, FEAT // 16, outer_step, 0)

    for i in range(PARTS):
        squares = gather(1, i, squares)
    sq[0] = squares
    q_copies = []
    for d, peer in enumerate((mate, across, diag)):
        q_copies.append(remote(sq.at[0], sq.at[1 + d], qsend_sem.at[d], qrecv_sem.at[d], peer))
        q_copies[-1].start()
    for copy in q_copies:
        copy.wait_recv()
    everything = jnp.sum(sq[0] + sq[1] + sq[2] + sq[3], keepdims=True)
    clip = jnp.minimum(1.0, CLIP / jnp.sqrt(everything + 1e-12))
    factor[...] = jnp.broadcast_to(clip, (8, HD))

    for j in range(2):
        for i in range(PARTS):

            def adam(s, _, j=j, i=i):
                at = pl.multiple_of(s * 16, 16)
                rows = pl.ds(pl.multiple_of(i * PROWS + s * 16, 16), 16)
                ratio = jnp.concatenate([factor[...]] * 2, axis=0)
                chosen_row = mask[rows, :]
                rate = jnp.where(chosen_row == j, alpha * LEARN_RATE, LEARN_RATE)
                for k in range(HALF // HD):
                    c = j * HALF + k * HD
                    clipped = gown[j, i, pl.ds(at, 16), k * HD : (k + 1) * HD] * ratio
                    one = BETA_ONE * first[rows, c : c + HD].astype(F32) + (1.0 - BETA_ONE) * clipped
                    two = (
                        BETA_TWO * second[rows, c : c + HD].astype(F32)
                        + (1.0 - BETA_TWO) * clipped * clipped
                    )
                    step = one / (jnp.sqrt(two) + ADAM_EPS)
                    new_weight[0, rows, c : c + HD] = (
                        level[rows, c : c + HD] - rate * step
                    ).astype(BF16)
                return 0

            lax.fori_loop(0, PROWS // 16, adam, 0, unroll=4)

    sent = w_copies + t_copies + y_copies + z_copies + [x_copy] + list(az_copies.values()) + ay_copies
    for copy in sent + p_copies + d_copies + g_copies + q_copies:
        copy.wait_send()


def local(*args):
    dma = pltpu.SemaphoreType.DMA
    any_space = pl.BlockSpec(memory_space=pl.ANY)
    vmem = pl.BlockSpec(memory_space=pltpu.VMEM)
    return pl.pallas_call(
        kernel,
        name="diloco_step",
        out_shape=(
            jax.ShapeDtypeStruct((1, FEAT, COLS), BF16),
            jax.ShapeDtypeStruct((FEAT, COLS), F32),
        ),
        in_specs=[any_space] * 9 + [pl.BlockSpec(memory_space=pltpu.SMEM)],
        out_specs=(vmem, vmem),
        scratch_shapes=[
            pltpu.SMEM((FEAT // ROWS,), jnp.int32),
            pltpu.SMEM((4,), F32),
            pltpu.VMEM((FEAT, COLS), BF16),
            pltpu.VMEM((2, FEAT, HALF), BF16),
            pltpu.VMEM((2, TOK, 2 * FEAT), BF16),
            pltpu.VMEM((2 * FEAT, 2 * TOK), BF16),
            pltpu.VMEM((2, 2, TOK, HALF), F32),
            pltpu.VMEM((TOK, COLS), BF16),
            pltpu.VMEM((FEAT, HD), jnp.int32),
            pltpu.VMEM((FEAT, HALF), BF16),
            pltpu.VMEM((NY - 1, YROWS, HALF), BF16),
            pltpu.VMEM((YROWS, HALF), F32),
            pltpu.VMEM((NZ - 1, ZROWS, HALF), F32),
            pltpu.VMEM((ZROWS, HALF), F32),
            pltpu.VMEM((ZROWS, HALF), F32),
            pltpu.VMEM((FEAT, HALF), F32),
            pltpu.VMEM((2, TOK, HALF), F32),
            pltpu.VMEM((2, TOK, HALF), F32),
            pltpu.VMEM((2, 2, TOK, HALF), BF16),
            pltpu.VMEM((2, PARTS, PROWS, HALF), BF16),
            pltpu.VMEM((2, PARTS, PROWS, HALF), BF16),
            pltpu.VMEM((2, PARTS, PROWS, HALF), F32),
            pltpu.VMEM((FEAT, COLS), BF16),
            pltpu.VMEM((FEAT, COLS), BF16),
            pltpu.VMEM((FEAT, COLS), BF16),
            pltpu.VMEM((FEAT, COLS), F32),
            pltpu.VMEM((FEAT, COLS), F32),
            pltpu.VMEM((8, HD), F32),
            pltpu.VMEM((4, 8, HD), F32),
            dma((2,)),
            dma((8,)),
            dma((2,)),
            dma((2,)),
            dma((2,)),
            dma((2,)),
            dma((NY - 1,)),
            dma((NY - 1,)),
            dma((NZ - 1,)),
            dma((NZ - 1,)),
            dma,
            dma,
            dma((NZ - 1,)),
            dma((NZ - 1,)),
            dma((NZ, NY - 1)),
            dma((NZ, NY - 1)),
            dma((2,)),
            dma((2,)),
            dma((2,)),
            dma((2,)),
            dma((2, PARTS)),
            dma((2, PARTS)),
            dma((3,)),
            dma((3,)),
        ],
        compiler_params=pltpu.CompilerParams(
            collective_id=0, has_side_effects=True, vmem_limit_bytes=40 * 2**20
        ),
    )(*[pltpu.with_memory_space_constraint(a, pltpu.HBM) for a in args[:9]], args[9])


def solution(mesh):
    placed = (
        P("rep", "fsdp", None),
        P("rep", "fsdp", None),
        P("rep", "fsdp", None),
        P("fsdp", None),
        P("fsdp", None),
        P("rep", "fsdp", None),
        P("rep", "fsdp", None),
        P("fsdp"),
        P(),
        P("rep"),
    )
    return jax.shard_map(
        local,
        mesh=mesh,
        in_specs=placed,
        out_specs=(P("rep", "fsdp", None), P("fsdp", None)),
        check_vma=False,
    )
```

```python
import functools

import jax
import jax.numpy as jnp
from jax import lax
from jax.experimental import pallas as pl
from jax.experimental.pallas import tpu as pltpu
from jax.sharding import PartitionSpec as P

HD = 128
ROWS = 8
EPS_NORM = 1e-06
BETA_ONE = 0.9
BETA_TWO = 0.999
ADAM_EPS = 1e-08
LEARN_RATE = 0.3
DECAY = 0.1
CLIP = 0.05
MOMENT_COEF = 0.9
OUTER_RATE = 0.7

MESH = pl.DeviceIdType.MESH
F32 = jnp.float32
BF16 = jnp.bfloat16

NY = 4
NZ = 8
REPS = 64
TOK = 384
FEAT = 1024
COLS = 512
HALF = 256
PARTS = 4
PROWS = FEAT // PARTS
YROWS = FEAT // NY
ZROWS = YROWS // NZ
NEAR = (1, 7, 2, 6, 3, 5, 4)


def place(x_lo, z, y, f):
    return (x_lo * (NZ * NY) + z * NY + y, f)


def kernel(
    weight,
    adam_first,
    adam_second,
    anchor,
    momentum,
    tokens,
    cotangent,
    plan_in,
    mix_weights_in,
    mix_index,
    new_weight,
    new_momentum,
    plan,
    mix_weights,
    wown,
    wrecv,
    tch,
    tt,
    begun,
    cot,
    mask,
    picked,
    yrecv,
    ysum,
    zrecv,
    zsum,
    xrecv,
    mean,
    psend,
    precv,
    dch,
    gsend,
    grecv,
    gown,
    first,
    second,
    base,
    old,
    level,
    factor,
    sq,
    ready_sem,
    small_sem,
    load_sem,
    wsend_sem,
    wrecv_sem,
    tsend_sem,
    trecv_sem,
    ysend_sem,
    yrecv_sem,
    zsend_sem,
    zrecv_sem,
    xsend_sem,
    xrecv_sem,
    azsend_sem,
    azrecv_sem,
    aysend_sem,
    ayrecv_sem,
    psend_sem,
    precv_sem,
    dsend_sem,
    drecv_sem,
    gsend_sem,
    grecv_sem,
    qsend_sem,
    qrecv_sem,
):
    rep = lax.axis_index("rep")
    f = lax.axis_index("fsdp")
    x_lo = rep // (NZ * NY)
    z = (rep // NY) % NZ
    y = rep % NY
    mate_f = f + 1 - 2 * (f % 2)
    across_f = (f + 2) % 4
    diag_f = 3 - f
    mate = (rep, mate_f)
    across = (rep, across_f)
    diag = (rep, diag_f)
    y_peers = [place(x_lo, z, (y + d) % NY, f) for d in range(1, NY)]
    z_peers = [place(x_lo, (z + d) % NZ, y, f) for d in range(1, NZ)]
    x_peer = place(1 - x_lo, z, y, f)

    barrier = pltpu.get_barrier_semaphore()
    peers = [across, mate, diag, x_peer] + y_peers
    for peer in peers:
        pl.semaphore_signal(barrier, inc=1, device_id=peer, device_id_type=MESH)
    for d in range(1, NZ):

        @pl.when((z + d) % NZ > z)
        def _(peer=z_peers[d - 1]):
            pl.semaphore_signal(barrier, inc=1, device_id=peer, device_id_type=MESH)

    def columns(index):
        return pl.ds(pl.multiple_of(index * FEAT, FEAT), FEAT)

    small = [
        pltpu.make_async_copy(plan_in, plan, small_sem.at[0]),
        pltpu.make_async_copy(mix_weights_in, mix_weights, small_sem.at[1]),
    ]
    for copy in small:
        copy.start()
    loads = [
        pltpu.make_async_copy(weight.at[0], wown, load_sem.at[0]),
        pltpu.make_async_copy(
            tokens.at[0, :, columns(f)], tch.at[0, :, pl.ds(0, FEAT)], load_sem.at[1]
        ),
        pltpu.make_async_copy(
            tokens.at[0, :, columns(across_f)], tch.at[0, :, pl.ds(FEAT, FEAT)], load_sem.at[2]
        ),
        pltpu.make_async_copy(cotangent.at[0], cot, load_sem.at[3]),
        pltpu.make_async_copy(anchor, base, load_sem.at[4]),
        pltpu.make_async_copy(momentum, old, load_sem.at[5]),
        pltpu.make_async_copy(adam_first.at[0], first, load_sem.at[6]),
        pltpu.make_async_copy(adam_second.at[0], second, load_sem.at[7]),
    ]
    for copy in loads:
        copy.start()

    pl.semaphore_wait(barrier, len(peers) + z)

    def remote(src, dst, send, recv, to):
        return pltpu.make_async_remote_copy(
            src_ref=src, dst_ref=dst, send_sem=send, recv_sem=recv, device_id=to, device_id_type=MESH
        )

    w_copies = [
        remote(
            weight.at[0, :, pl.ds(j * HALF, HALF)], wrecv.at[j], wsend_sem.at[j], wrecv_sem.at[j], across
        )
        for j in range(2)
    ]
    for copy in w_copies:
        copy.start()
    t_copies = [
        remote(
            tokens.at[0, :, columns(index)],
            tch.at[1, :, pl.ds(b * FEAT, FEAT)],
            tsend_sem.at[b],
            trecv_sem.at[b],
            mate,
        )
        for b, index in enumerate((mate_f, diag_f))
    ]
    for copy in t_copies:
        copy.start()
    for d in range(1, NZ):

        @pl.when((z + d) % NZ < z)
        def _(peer=z_peers[d - 1]):
            pl.semaphore_signal(ready_sem, inc=1, device_id=peer, device_id_type=MESH)


    for copy in small:
        copy.wait()

    def mark(i, _):
        mask[pl.ds(pl.multiple_of(i * ROWS, ROWS), ROWS), :] = jnp.full((ROWS, HD), plan[i], jnp.int32)
        return 0

    lax.fori_loop(0, FEAT // ROWS, mark, 0, unroll=8)

    loads[0].wait()

    def pick(start):
        def body(i, _):
            rows = pl.ds(pl.multiple_of(start + i * 32, 32), 32)
            chosen = mask[rows, :] == 0
            for k in range(HALF // HD):
                low = wown[rows, k * HD : (k + 1) * HD].astype(F32)
                high = wown[rows, HALF + k * HD : HALF + (k + 1) * HD].astype(F32)
                picked[rows, k * HD : (k + 1) * HD] = jnp.where(chosen, low, high).astype(BF16)
            return 0

        lax.fori_loop(0, YROWS // 64, body, 0, unroll=2)

    y_copies = [[], []]
    for part in range(2):
        for d in range(1, NY):
            start = ((y + d) % NY) * YROWS + part * (YROWS // 2)
            pick(start)
            copy = remote(
                picked.at[pl.ds(pl.multiple_of(start, YROWS // 2), YROWS // 2)],
                yrecv.at[d - 1, pl.ds(part * (YROWS // 2), YROWS // 2)],
                ysend_sem.at[d - 1, part],
                yrecv_sem.at[d - 1, part],
                y_peers[d - 1],
            )
            copy.start()
            y_copies[part].append(copy)
        pick(y * YROWS + part * (YROWS // 2))

    def turn(t):
        def body(i, _):
            at = pl.multiple_of(i * HD, HD)
            tt[pl.ds(at, HD), t * TOK : (t + 1) * TOK] = tch[t, :, pl.ds(at, HD)].T
            return 0

        lax.fori_loop(0, 2 * FEAT // HD, body, 0)

    loads[1].wait()
    loads[2].wait()
    turn(0)

    for copy in t_copies:
        copy.wait_recv()
    turn(1)
    def add_y(i, _):
        at = pl.multiple_of(i * 32, 32)
        rows = pl.ds(at, 32)
        total = picked[pl.ds(pl.multiple_of(y * YROWS + i * 32, 32), 32), :].astype(F32)
        for d in range(NY - 1):
            total = total + yrecv[d, rows, :].astype(F32)
        ysum[rows, :] = total
        return 0

    z_copies = []
    for d in range(1, NZ):
        start = pl.multiple_of(((z + d) % NZ) * ZROWS, ZROWS)
        z_copies.append(
            remote(
                ysum.at[pl.ds(start, ZROWS)],
                zrecv.at[d - 1],
                zsend_sem.at[d - 1],
                zrecv_sem.at[d - 1],
                z_peers[d - 1],
            )
        )
    for part in range(2):
        for copy in y_copies[part]:
            copy.wait_recv()
        lax.fori_loop(part * NZ // 2, (part + 1) * NZ // 2, add_y, 0)
        if part == 0:

            @pl.when(z < NZ - 1)
            def _():
                pl.semaphore_wait(ready_sem, NZ - 1 - z)

        for d in range(1, NZ):
            pl.when(((z + d) % NZ) // (NZ // 2) == part)(z_copies[d - 1].start)

    loads[3].wait()

    own_block = pl.ds(0, FEAT)
    across_block = pl.ds(FEAT, FEAT)
    p_copies = []
    d_copies = []
    g_copies = []

    def prepare(t, j):
        begun[t, j] = jnp.dot(
            tch[t, :, own_block], wown[:, j * HALF : (j + 1) * HALF], preferred_element_type=F32
        )

    def project(t, j):
        return begun[t, j] + jnp.dot(tch[t, :, across_block], wrecv[j], preferred_element_type=F32)

    def add_z():
        for copy in z_copies:
            copy.wait_recv()
        total = ysum[pl.ds(pl.multiple_of(z * ZROWS, ZROWS), ZROWS), :]
        for d in range(NZ - 1):
            total = total + zrecv[d]
        zsum[...] = total
        x_copy.start()

    def slice_of(d):
        start = y * YROWS + ((z + NZ - d) % NZ) * ZROWS
        return pl.ds(pl.multiple_of(start, ZROWS), ZROWS)

    def spread(d):
        rows = slice_of(d)
        for e in range(NY - 1):
            copy = remote(
                mean.at[rows], mean.at[rows], aysend_sem.at[d, e], ayrecv_sem.at[d, e], y_peers[e]
            )
            copy.start()
            ay_copies.append(copy)

    def add_x():
        x_copy.wait_recv()
        rows = slice_of(0)
        mean[rows, :] = (zsum[...] + xrecv[...]) * (1.0 / REPS)
        for d in NEAR:
            az_copies[d] = remote(
                mean.at[rows], mean.at[rows], azsend_sem.at[d - 1], azrecv_sem.at[d - 1], z_peers[d - 1]
            )
            az_copies[d].start()
        spread(0)

    def forward(*steps):
        for d in steps:
            az_copies[d].wait_recv()
            spread(d)

    x_copy = remote(zsum, xrecv, xsend_sem, xrecv_sem, x_peer)
    az_copies = {}
    ay_copies = []

    def chunk(j):
        w_copies[j].wait_recv()
        psend[j] = project(1, j)
        p_copy = remote(psend.at[j], precv.at[j], psend_sem.at[j], precv_sem.at[j], mate)
        p_copy.start()
        p_copies.append(p_copy)
        keys = project(0, j)
        p_copy.wait_recv()
        keys = keys + precv[j]
        for k in range(HALF // HD):
            at = j * HALF + k * HD
            head = keys[:, k * HD : (k + 1) * HD]
            pull = cot[:, at : at + HD].astype(F32)
            scale = lax.rsqrt(jnp.sum(head * head, axis=1, keepdims=True) * (1.0 / HD) + EPS_NORM)
            inner = jnp.sum(head * pull, axis=1, keepdims=True) * (1.0 / HD)
            back = scale * (pull - head * (scale * scale * inner))
            dch[j, 0, :, k * HD : (k + 1) * HD] = back.astype(BF16)
        d_copy = remote(dch.at[j, 0], dch.at[j, 1], dsend_sem.at[j], drecv_sem.at[j], mate)
        d_copy.start()
        d_copies.append(d_copy)
        if j == 0:
            add_z()
        d_copy.wait_recv()

        def grad(at):
            low = jnp.dot(tt[pl.ds(at, PROWS), 0:TOK], dch[j, 0], preferred_element_type=F32)
            high = jnp.dot(
                tt[pl.ds(at, PROWS), TOK : 2 * TOK], dch[j, 1], preferred_element_type=F32
            )
            return low + high

        for i in range(PARTS):
            gsend[j, i] = grad(FEAT + i * PROWS).astype(BF16)
            g_copy = remote(
                gsend.at[j, i], grecv.at[j, i], gsend_sem.at[j, i], grecv_sem.at[j, i], across
            )
            g_copy.start()
            g_copies.append(g_copy)
        for i in range(PARTS):
            gown[j, i] = grad(i * PROWS)

    for t in range(2):
        for j in range(2):
            prepare(t, j)

    chunk(0)
    add_x()
    chunk(1)
    forward(*NEAR)

    def gather(j, i, total):
        g_copies[j * PARTS + i].wait_recv()

        def body(s, total):
            rows = pl.ds(pl.multiple_of(s * 32, 32), 32)
            grad = (gown[j, i, rows, :] + grecv[j, i, rows, :].astype(F32)) * (1.0 / (4 * TOK))
            gown[j, i, rows, :] = grad
            square = grad * grad
            for r in range(4):
                for k in range(HALF // HD):
                    total = total + square[r * 8 : (r + 1) * 8, k * HD : (k + 1) * HD]
            return total

        return lax.fori_loop(0, PROWS // 32, body, total, unroll=2)

    squares = jnp.zeros((8, HD), F32)
    for i in range(PARTS):
        squares = gather(0, i, squares)

    for copy in loads[4:]:
        copy.wait()
    choice = mix_index[0]
    alpha = mix_weights[0]
    for k in range(1, 4):
        alpha = jnp.where(choice == k, mix_weights[k], alpha)
    for copy in ay_copies:
        copy.wait_recv()

    def outer_step(i, _):
        rows = pl.ds(pl.multiple_of(i * 16, 16), 16)
        row_frag = mask[rows, :]
        for k in range(HALF // HD):
            middle = mean[rows, k * HD : (k + 1) * HD]
            for index in range(2):
                at = index * HALF + k * HD
                chosen = row_frag == index
                start = base[rows, at : at + HD].astype(F32)
                wide = wown[rows, at : at + HD].astype(F32) * (1.0 - LEARN_RATE * DECAY)
                before = old[rows, at : at + HD]
                average = start - middle
                moved = MOMENT_COEF * before + average
                outer = start - OUTER_RATE * (average + MOMENT_COEF * moved)
                new_momentum[rows, at : at + HD] = jnp.where(chosen, moved, before)
                level[rows, at : at + HD] = jnp.where(
                    chosen, alpha * wide + (1.0 - alpha) * outer, wide
                )
        return 0

    lax.fori_loop(0, FEAT // 16, outer_step, 0)

    for i in range(PARTS):
        squares = gather(1, i, squares)
    sq[0] = squares
    q_copies = []
    for d, peer in enumerate((mate, across, diag)):
        q_copies.append(remote(sq.at[0], sq.at[1 + d], qsend_sem.at[d], qrecv_sem.at[d], peer))
        q_copies[-1].start()
    for copy in q_copies:
        copy.wait_recv()
    everything = jnp.sum(sq[0] + sq[1] + sq[2] + sq[3], keepdims=True)
    clip = jnp.minimum(1.0, CLIP / jnp.sqrt(everything + 1e-12))
    factor[...] = jnp.broadcast_to(clip, (8, HD))

    for j in range(2):
        for i in range(PARTS):

            def adam(s, _, j=j, i=i):
                at = pl.multiple_of(s * 16, 16)
                rows = pl.ds(pl.multiple_of(i * PROWS + s * 16, 16), 16)
                ratio = jnp.concatenate([factor[...]] * 2, axis=0)
                chosen_row = mask[rows, :]
                rate = jnp.where(chosen_row == j, alpha * LEARN_RATE, LEARN_RATE)
                for k in range(HALF // HD):
                    c = j * HALF + k * HD
                    clipped = gown[j, i, pl.ds(at, 16), k * HD : (k + 1) * HD] * ratio
                    one = BETA_ONE * first[rows, c : c + HD].astype(F32) + (1.0 - BETA_ONE) * clipped
                    two = (
                        BETA_TWO * second[rows, c : c + HD].astype(F32)
                        + (1.0 - BETA_TWO) * clipped * clipped
                    )
                    step = one / (jnp.sqrt(two) + ADAM_EPS)
                    new_weight[0, rows, c : c + HD] = (
                        level[rows, c : c + HD] - rate * step
                    ).astype(BF16)
                return 0

            lax.fori_loop(0, PROWS // 16, adam, 0, unroll=4)

    sent = w_copies + t_copies + y_copies[0] + y_copies[1] + z_copies + [x_copy] + list(az_copies.values()) + ay_copies
    for copy in sent + p_copies + d_copies + g_copies + q_copies:
        copy.wait_send()


def local(*args):
    dma = pltpu.SemaphoreType.DMA
    any_space = pl.BlockSpec(memory_space=pl.ANY)
    vmem = pl.BlockSpec(memory_space=pltpu.VMEM)
    return pl.pallas_call(
        kernel,
        name="diloco_step",
        out_shape=(
            jax.ShapeDtypeStruct((1, FEAT, COLS), BF16),
            jax.ShapeDtypeStruct((FEAT, COLS), F32),
        ),
        in_specs=[any_space] * 9 + [pl.BlockSpec(memory_space=pltpu.SMEM)],
        out_specs=(vmem, vmem),
        scratch_shapes=[
            pltpu.SMEM((FEAT // ROWS,), jnp.int32),
            pltpu.SMEM((4,), F32),
            pltpu.VMEM((FEAT, COLS), BF16),
            pltpu.VMEM((2, FEAT, HALF), BF16),
            pltpu.VMEM((2, TOK, 2 * FEAT), BF16),
            pltpu.VMEM((2 * FEAT, 2 * TOK), BF16),
            pltpu.VMEM((2, 2, TOK, HALF), F32),
            pltpu.VMEM((TOK, COLS), BF16),
            pltpu.VMEM((FEAT, HD), jnp.int32),
            pltpu.VMEM((FEAT, HALF), BF16),
            pltpu.VMEM((NY - 1, YROWS, HALF), BF16),
            pltpu.VMEM((YROWS, HALF), F32),
            pltpu.VMEM((NZ - 1, ZROWS, HALF), F32),
            pltpu.VMEM((ZROWS, HALF), F32),
            pltpu.VMEM((ZROWS, HALF), F32),
            pltpu.VMEM((FEAT, HALF), F32),
            pltpu.VMEM((2, TOK, HALF), F32),
            pltpu.VMEM((2, TOK, HALF), F32),
            pltpu.VMEM((2, 2, TOK, HALF), BF16),
            pltpu.VMEM((2, PARTS, PROWS, HALF), BF16),
            pltpu.VMEM((2, PARTS, PROWS, HALF), BF16),
            pltpu.VMEM((2, PARTS, PROWS, HALF), F32),
            pltpu.VMEM((FEAT, COLS), BF16),
            pltpu.VMEM((FEAT, COLS), BF16),
            pltpu.VMEM((FEAT, COLS), BF16),
            pltpu.VMEM((FEAT, COLS), F32),
            pltpu.VMEM((FEAT, COLS), F32),
            pltpu.VMEM((8, HD), F32),
            pltpu.VMEM((4, 8, HD), F32),
            pltpu.SemaphoreType.REGULAR,
            dma((2,)),
            dma((8,)),
            dma((2,)),
            dma((2,)),
            dma((2,)),
            dma((2,)),
            dma((NY - 1, 2)),
            dma((NY - 1, 2)),
            dma((NZ - 1,)),
            dma((NZ - 1,)),
            dma,
            dma,
            dma((NZ - 1,)),
            dma((NZ - 1,)),
            dma((NZ, NY - 1)),
            dma((NZ, NY - 1)),
            dma((2,)),
            dma((2,)),
            dma((2,)),
            dma((2,)),
            dma((2, PARTS)),
            dma((2, PARTS)),
            dma((3,)),
            dma((3,)),
        ],
        compiler_params=pltpu.CompilerParams(
            collective_id=0, has_side_effects=True, vmem_limit_bytes=40 * 2**20
        ),
    )(*[pltpu.with_memory_space_constraint(a, pltpu.HBM) for a in args[:9]], args[9])


def solution(mesh):
    placed = (
        P("rep", "fsdp", None),
        P("rep", "fsdp", None),
        P("rep", "fsdp", None),
        P("fsdp", None),
        P("fsdp", None),
        P("rep", "fsdp", None),
        P("rep", "fsdp", None),
        P("fsdp"),
        P(),
        P("rep"),
    )
    return jax.shard_map(
        local,
        mesh=mesh,
        in_specs=placed,
        out_specs=(P("rep", "fsdp", None), P("fsdp", None)),
        check_vma=False,
    )
```

```python
import functools

import jax
import jax.numpy as jnp
from jax import lax
from jax.experimental import pallas as pl
from jax.experimental.pallas import tpu as pltpu
from jax.sharding import PartitionSpec as P

HD = 128
ROWS = 8
EPS_NORM = 1e-06
BETA_ONE = 0.9
BETA_TWO = 0.999
ADAM_EPS = 1e-08
LEARN_RATE = 0.3
DECAY = 0.1
CLIP = 0.05
MOMENT_COEF = 0.9
OUTER_RATE = 0.7

MESH = pl.DeviceIdType.MESH
F32 = jnp.float32
BF16 = jnp.bfloat16

NY = 4
NZ = 8
REPS = 64
TOK = 384
FEAT = 1024
COLS = 512
HALF = 256
PARTS = 4
PROWS = FEAT // PARTS
YROWS = FEAT // NY
ZROWS = YROWS // NZ
NEAR = (1, 7, 2, 6, 3, 5, 4)


def place(x_lo, z, y, f):
    return (x_lo * (NZ * NY) + z * NY + y, f)


def kernel(
    weight,
    adam_first,
    adam_second,
    anchor,
    momentum,
    tokens,
    cotangent,
    plan_in,
    mix_weights_in,
    mix_index,
    linear,
    square,
    total_squares,
    level,
    moved_out,
    rate,
    kept_first,
    kept_second,
    plan,
    mix_weights,
    wown,
    wrecv,
    tch,
    tt,
    begun,
    cot,
    mask,
    picked,
    yrecv,
    ysum,
    zrecv,
    zsum,
    xrecv,
    mean,
    psend,
    precv,
    dch,
    gsend,
    grecv,
    gown,
    first,
    second,
    base,
    old,
    sq,
    ready_sem,
    small_sem,
    load_sem,
    wsend_sem,
    wrecv_sem,
    tsend_sem,
    trecv_sem,
    ysend_sem,
    yrecv_sem,
    zsend_sem,
    zrecv_sem,
    xsend_sem,
    xrecv_sem,
    azsend_sem,
    azrecv_sem,
    aysend_sem,
    ayrecv_sem,
    psend_sem,
    precv_sem,
    dsend_sem,
    drecv_sem,
    gsend_sem,
    grecv_sem,
    qsend_sem,
    qrecv_sem,
):
    rep = lax.axis_index("rep")
    f = lax.axis_index("fsdp")
    x_lo = rep // (NZ * NY)
    z = (rep // NY) % NZ
    y = rep % NY
    mate_f = f + 1 - 2 * (f % 2)
    across_f = (f + 2) % 4
    diag_f = 3 - f
    mate = (rep, mate_f)
    across = (rep, across_f)
    diag = (rep, diag_f)
    y_peers = [place(x_lo, z, (y + d) % NY, f) for d in range(1, NY)]
    z_peers = [place(x_lo, (z + d) % NZ, y, f) for d in range(1, NZ)]
    x_peer = place(1 - x_lo, z, y, f)

    barrier = pltpu.get_barrier_semaphore()
    peers = [across, mate, diag, x_peer] + y_peers
    for peer in peers:
        pl.semaphore_signal(barrier, inc=1, device_id=peer, device_id_type=MESH)
    for d in range(1, NZ):

        @pl.when((z + d) % NZ > z)
        def _(peer=z_peers[d - 1]):
            pl.semaphore_signal(barrier, inc=1, device_id=peer, device_id_type=MESH)

    def columns(index):
        return pl.ds(pl.multiple_of(index * FEAT, FEAT), FEAT)

    small = [
        pltpu.make_async_copy(plan_in, plan, small_sem.at[0]),
        pltpu.make_async_copy(mix_weights_in, mix_weights, small_sem.at[1]),
    ]
    for copy in small:
        copy.start()
    loads = [
        pltpu.make_async_copy(weight.at[0], wown, load_sem.at[0]),
        pltpu.make_async_copy(
            tokens.at[0, :, columns(f)], tch.at[0, :, pl.ds(0, FEAT)], load_sem.at[1]
        ),
        pltpu.make_async_copy(
            tokens.at[0, :, columns(across_f)], tch.at[0, :, pl.ds(FEAT, FEAT)], load_sem.at[2]
        ),
        pltpu.make_async_copy(cotangent.at[0], cot, load_sem.at[3]),
        pltpu.make_async_copy(anchor, base, load_sem.at[4]),
        pltpu.make_async_copy(momentum, old, load_sem.at[5]),
        pltpu.make_async_copy(adam_first.at[0], first, load_sem.at[6]),
        pltpu.make_async_copy(adam_second.at[0], second, load_sem.at[7]),
    ]
    for copy in loads:
        copy.start()

    pl.semaphore_wait(barrier, len(peers) + z)

    def remote(src, dst, send, recv, to):
        return pltpu.make_async_remote_copy(
            src_ref=src, dst_ref=dst, send_sem=send, recv_sem=recv, device_id=to, device_id_type=MESH
        )

    w_copies = [
        remote(
            weight.at[0, :, pl.ds(j * HALF, HALF)], wrecv.at[j], wsend_sem.at[j], wrecv_sem.at[j], across
        )
        for j in range(2)
    ]
    for copy in w_copies:
        copy.start()
    t_copies = [
        remote(
            tokens.at[0, :, columns(index)],
            tch.at[1, :, pl.ds(b * FEAT, FEAT)],
            tsend_sem.at[b],
            trecv_sem.at[b],
            mate,
        )
        for b, index in enumerate((mate_f, diag_f))
    ]
    for copy in t_copies:
        copy.start()
    for d in range(1, NZ):

        @pl.when((z + d) % NZ < z)
        def _(peer=z_peers[d - 1]):
            pl.semaphore_signal(ready_sem, inc=1, device_id=peer, device_id_type=MESH)


    for copy in small:
        copy.wait()

    def mark(i, _):
        mask[pl.ds(pl.multiple_of(i * ROWS, ROWS), ROWS), :] = jnp.full((ROWS, HD), plan[i], jnp.int32)
        return 0

    lax.fori_loop(0, FEAT // ROWS, mark, 0, unroll=8)

    loads[0].wait()

    def pick(start):
        def body(i, _):
            rows = pl.ds(pl.multiple_of(start + i * 32, 32), 32)
            chosen = mask[rows, :] == 0
            for k in range(HALF // HD):
                low = wown[rows, k * HD : (k + 1) * HD].astype(F32)
                high = wown[rows, HALF + k * HD : HALF + (k + 1) * HD].astype(F32)
                picked[rows, k * HD : (k + 1) * HD] = jnp.where(chosen, low, high).astype(BF16)
            return 0

        lax.fori_loop(0, YROWS // 64, body, 0, unroll=2)

    y_copies = [[], []]
    for part in range(2):
        for d in range(1, NY):
            start = ((y + d) % NY) * YROWS + part * (YROWS // 2)
            pick(start)
            copy = remote(
                picked.at[pl.ds(pl.multiple_of(start, YROWS // 2), YROWS // 2)],
                yrecv.at[d - 1, pl.ds(part * (YROWS // 2), YROWS // 2)],
                ysend_sem.at[d - 1, part],
                yrecv_sem.at[d - 1, part],
                y_peers[d - 1],
            )
            copy.start()
            y_copies[part].append(copy)
        pick(y * YROWS + part * (YROWS // 2))

    def turn(t):
        def body(i, _):
            at = pl.multiple_of(i * HD, HD)
            tt[pl.ds(at, HD), t * TOK : (t + 1) * TOK] = tch[t, :, pl.ds(at, HD)].T
            return 0

        lax.fori_loop(0, 2 * FEAT // HD, body, 0)

    loads[1].wait()
    loads[2].wait()
    turn(0)

    for copy in t_copies:
        copy.wait_recv()
    turn(1)
    def add_y(i, _):
        at = pl.multiple_of(i * 32, 32)
        rows = pl.ds(at, 32)
        total = picked[pl.ds(pl.multiple_of(y * YROWS + i * 32, 32), 32), :].astype(F32)
        for d in range(NY - 1):
            total = total + yrecv[d, rows, :].astype(F32)
        ysum[rows, :] = total
        return 0

    z_copies = []
    for d in range(1, NZ):
        start = pl.multiple_of(((z + d) % NZ) * ZROWS, ZROWS)
        z_copies.append(
            remote(
                ysum.at[pl.ds(start, ZROWS)],
                zrecv.at[d - 1],
                zsend_sem.at[d - 1],
                zrecv_sem.at[d - 1],
                z_peers[d - 1],
            )
        )
    for part in range(2):
        for copy in y_copies[part]:
            copy.wait_recv()
        lax.fori_loop(part * NZ // 2, (part + 1) * NZ // 2, add_y, 0)
        if part == 0:

            @pl.when(z < NZ - 1)
            def _():
                pl.semaphore_wait(ready_sem, NZ - 1 - z)

        for d in range(1, NZ):
            pl.when(((z + d) % NZ) // (NZ // 2) == part)(z_copies[d - 1].start)

    loads[3].wait()

    own_block = pl.ds(0, FEAT)
    across_block = pl.ds(FEAT, FEAT)
    p_copies = []
    d_copies = []
    g_copies = []

    def prepare(t, j):
        begun[t, j] = jnp.dot(
            tch[t, :, own_block], wown[:, j * HALF : (j + 1) * HALF], preferred_element_type=F32
        )

    def project(t, j):
        return begun[t, j] + jnp.dot(tch[t, :, across_block], wrecv[j], preferred_element_type=F32)

    def add_z():
        for copy in z_copies:
            copy.wait_recv()
        total = ysum[pl.ds(pl.multiple_of(z * ZROWS, ZROWS), ZROWS), :]
        for d in range(NZ - 1):
            total = total + zrecv[d]
        zsum[...] = total
        x_copy.start()

    def slice_of(d):
        start = y * YROWS + ((z + NZ - d) % NZ) * ZROWS
        return pl.ds(pl.multiple_of(start, ZROWS), ZROWS)

    def spread(d):
        rows = slice_of(d)
        for e in range(NY - 1):
            copy = remote(
                mean.at[rows], mean.at[rows], aysend_sem.at[d, e], ayrecv_sem.at[d, e], y_peers[e]
            )
            copy.start()
            ay_copies.append(copy)

    def add_x():
        x_copy.wait_recv()
        rows = slice_of(0)
        mean[rows, :] = (zsum[...] + xrecv[...]) * (1.0 / REPS)
        for d in NEAR:
            az_copies[d] = remote(
                mean.at[rows], mean.at[rows], azsend_sem.at[d - 1], azrecv_sem.at[d - 1], z_peers[d - 1]
            )
            az_copies[d].start()
        spread(0)

    def forward(*steps):
        for d in steps:
            az_copies[d].wait_recv()
            spread(d)

    x_copy = remote(zsum, xrecv, xsend_sem, xrecv_sem, x_peer)
    az_copies = {}
    ay_copies = []

    def chunk(j):
        w_copies[j].wait_recv()
        psend[j] = project(1, j)
        p_copy = remote(psend.at[j], precv.at[j], psend_sem.at[j], precv_sem.at[j], mate)
        p_copy.start()
        p_copies.append(p_copy)
        keys = project(0, j)
        p_copy.wait_recv()
        keys = keys + precv[j]
        for k in range(HALF // HD):
            at = j * HALF + k * HD
            head = keys[:, k * HD : (k + 1) * HD]
            pull = cot[:, at : at + HD].astype(F32)
            scale = lax.rsqrt(jnp.sum(head * head, axis=1, keepdims=True) * (1.0 / HD) + EPS_NORM)
            inner = jnp.sum(head * pull, axis=1, keepdims=True) * (1.0 / HD)
            back = scale * (pull - head * (scale * scale * inner))
            dch[j, 0, :, k * HD : (k + 1) * HD] = back.astype(BF16)
        d_copy = remote(dch.at[j, 0], dch.at[j, 1], dsend_sem.at[j], drecv_sem.at[j], mate)
        d_copy.start()
        d_copies.append(d_copy)
        if j == 0:
            add_z()
        d_copy.wait_recv()

        def grad(at):
            low = jnp.dot(tt[pl.ds(at, PROWS), 0:TOK], dch[j, 0], preferred_element_type=F32)
            high = jnp.dot(
                tt[pl.ds(at, PROWS), TOK : 2 * TOK], dch[j, 1], preferred_element_type=F32
            )
            return low + high

        for i in range(PARTS):
            gsend[j, i] = grad(FEAT + i * PROWS).astype(BF16)
            g_copy = remote(
                gsend.at[j, i], grecv.at[j, i], gsend_sem.at[j, i], grecv_sem.at[j, i], across
            )
            g_copy.start()
            g_copies.append(g_copy)
        for i in range(PARTS):
            gown[j, i] = grad(i * PROWS)

    for t in range(2):
        for j in range(2):
            prepare(t, j)

    chunk(0)
    add_x()
    chunk(1)
    forward(*NEAR)

    def gather(j, i, total):
        g_copies[j * PARTS + i].wait_recv()

        def body(s, total):
            rows = pl.ds(pl.multiple_of(s * 32, 32), 32)
            grad = (gown[j, i, rows, :] + grecv[j, i, rows, :].astype(F32)) * (1.0 / (4 * TOK))
            linear[j, i, rows, :] = (1.0 - BETA_ONE) * grad
            power = grad * grad
            square[j, i, rows, :] = (1.0 - BETA_TWO) * power
            for r in range(4):
                for k in range(HALF // HD):
                    total = total + power[r * 8 : (r + 1) * 8, k * HD : (k + 1) * HD]
            return total

        return lax.fori_loop(0, PROWS // 32, body, total, unroll=2)

    squares = jnp.zeros((8, HD), F32)
    for i in range(PARTS):
        squares = gather(0, i, squares)

    for copy in loads[4:]:
        copy.wait()

    def decay(i, _):
        rows = pl.ds(pl.multiple_of(i * 16, 16), 16)
        kept_first[rows, :] = BETA_ONE * first[rows, :].astype(F32)
        kept_second[rows, :] = BETA_TWO * second[rows, :].astype(F32)
        return 0

    lax.fori_loop(0, FEAT // 16, decay, 0)
    choice = mix_index[0]
    alpha = mix_weights[0]
    for k in range(1, 4):
        alpha = jnp.where(choice == k, mix_weights[k], alpha)
    for copy in ay_copies:
        copy.wait_recv()

    def outer_step(i, _):
        rows = pl.ds(pl.multiple_of(i * 16, 16), 16)
        row_frag = mask[rows, :]
        for index in range(2):
            rate[index, rows, :] = jnp.where(row_frag == index, alpha * LEARN_RATE, LEARN_RATE)
        for k in range(HALF // HD):
            middle = mean[rows, k * HD : (k + 1) * HD]
            for index in range(2):
                at = index * HALF + k * HD
                chosen = row_frag == index
                start = base[rows, at : at + HD].astype(F32)
                wide = wown[rows, at : at + HD].astype(F32) * (1.0 - LEARN_RATE * DECAY)
                before = old[rows, at : at + HD]
                average = start - middle
                moved = MOMENT_COEF * before + average
                outer = start - OUTER_RATE * (average + MOMENT_COEF * moved)
                moved_out[rows, at : at + HD] = jnp.where(chosen, moved, before)
                level[rows, at : at + HD] = jnp.where(
                    chosen, alpha * wide + (1.0 - alpha) * outer, wide
                )
        return 0

    lax.fori_loop(0, FEAT // 16, outer_step, 0)

    for i in range(PARTS):
        squares = gather(1, i, squares)
    sq[0] = squares
    q_copies = []
    for d, peer in enumerate((mate, across, diag)):
        q_copies.append(remote(sq.at[0], sq.at[1 + d], qsend_sem.at[d], qrecv_sem.at[d], peer))
        q_copies[-1].start()
    for copy in q_copies:
        copy.wait_recv()
    total_squares[...] = sq[0] + sq[1] + sq[2] + sq[3]

    sent = w_copies + t_copies + y_copies[0] + y_copies[1] + z_copies + [x_copy] + list(az_copies.values()) + ay_copies
    for copy in sent + p_copies + d_copies + g_copies + q_copies:
        copy.wait_send()


def update(
    linear,
    square,
    total_squares,
    level,
    moved,
    rate,
    kept_first,
    kept_second,
    new_weight,
    new_momentum,
    result,
    weight_sem,
    momentum_sem,
):
    momentum_copy = pltpu.make_async_copy(moved, new_momentum, momentum_sem)
    momentum_copy.start()
    everything = jnp.sum(total_squares[...], keepdims=True)
    clip = jnp.minimum(1.0, CLIP / jnp.sqrt(everything + 1e-12))
    ratio = jnp.broadcast_to(clip, (16, HD))
    ratio_squared = ratio * ratio
    copies = []
    for i in range(PARTS):

        def adam(s, _, i=i):
            at = pl.multiple_of(s * 16, 16)
            rows = pl.ds(pl.multiple_of(i * PROWS + s * 16, 16), 16)
            for j in range(2):
                speed = rate[j, rows, :]
                for k in range(HALF // HD):
                    c = j * HALF + k * HD
                    block = (j, i, pl.ds(at, 16), slice(k * HD, (k + 1) * HD))
                    one = kept_first[rows, c : c + HD] + linear[block] * ratio
                    two = kept_second[rows, c : c + HD] + square[block] * ratio_squared
                    step = one / (two * lax.rsqrt(two) + ADAM_EPS)
                    result[rows, c : c + HD] = (level[rows, c : c + HD] - speed * step).astype(BF16)
            return 0

        lax.fori_loop(0, PROWS // 16, adam, 0, unroll=4)
        block = pl.ds(i * PROWS, PROWS)
        copy = pltpu.make_async_copy(result.at[block], new_weight.at[0, block], weight_sem.at[i])
        copy.start()
        copies.append(copy)
    for copy in copies:
        copy.wait()
    momentum_copy.wait()


def local(*args):
    dma = pltpu.SemaphoreType.DMA
    any_space = pl.BlockSpec(memory_space=pl.ANY)
    vmem = pl.BlockSpec(memory_space=pltpu.VMEM)
    parts = pl.pallas_call(
        kernel,
        name="diloco_step",
        out_shape=(
            jax.ShapeDtypeStruct((2, PARTS, PROWS, HALF), F32),
            jax.ShapeDtypeStruct((2, PARTS, PROWS, HALF), F32),
            jax.ShapeDtypeStruct((8, HD), F32),
            jax.ShapeDtypeStruct((FEAT, COLS), F32),
            jax.ShapeDtypeStruct((FEAT, COLS), F32),
            jax.ShapeDtypeStruct((2, FEAT, HD), F32),
            jax.ShapeDtypeStruct((FEAT, COLS), F32),
            jax.ShapeDtypeStruct((FEAT, COLS), F32),
        ),
        in_specs=[any_space] * 9 + [pl.BlockSpec(memory_space=pltpu.SMEM)],
        out_specs=(vmem,) * 8,
        scratch_shapes=[
            pltpu.SMEM((FEAT // ROWS,), jnp.int32),
            pltpu.SMEM((4,), F32),
            pltpu.VMEM((FEAT, COLS), BF16),
            pltpu.VMEM((2, FEAT, HALF), BF16),
            pltpu.VMEM((2, TOK, 2 * FEAT), BF16),
            pltpu.VMEM((2 * FEAT, 2 * TOK), BF16),
            pltpu.VMEM((2, 2, TOK, HALF), F32),
            pltpu.VMEM((TOK, COLS), BF16),
            pltpu.VMEM((FEAT, HD), jnp.int32),
            pltpu.VMEM((FEAT, HALF), BF16),
            pltpu.VMEM((NY - 1, YROWS, HALF), BF16),
            pltpu.VMEM((YROWS, HALF), F32),
            pltpu.VMEM((NZ - 1, ZROWS, HALF), F32),
            pltpu.VMEM((ZROWS, HALF), F32),
            pltpu.VMEM((ZROWS, HALF), F32),
            pltpu.VMEM((FEAT, HALF), F32),
            pltpu.VMEM((2, TOK, HALF), F32),
            pltpu.VMEM((2, TOK, HALF), F32),
            pltpu.VMEM((2, 2, TOK, HALF), BF16),
            pltpu.VMEM((2, PARTS, PROWS, HALF), BF16),
            pltpu.VMEM((2, PARTS, PROWS, HALF), BF16),
            pltpu.VMEM((2, PARTS, PROWS, HALF), F32),
            pltpu.VMEM((FEAT, COLS), BF16),
            pltpu.VMEM((FEAT, COLS), BF16),
            pltpu.VMEM((FEAT, COLS), BF16),
            pltpu.VMEM((FEAT, COLS), F32),
            pltpu.VMEM((4, 8, HD), F32),
            pltpu.SemaphoreType.REGULAR,
            dma((2,)),
            dma((8,)),
            dma((2,)),
            dma((2,)),
            dma((2,)),
            dma((2,)),
            dma((NY - 1, 2)),
            dma((NY - 1, 2)),
            dma((NZ - 1,)),
            dma((NZ - 1,)),
            dma,
            dma,
            dma((NZ - 1,)),
            dma((NZ - 1,)),
            dma((NZ, NY - 1)),
            dma((NZ, NY - 1)),
            dma((2,)),
            dma((2,)),
            dma((2,)),
            dma((2,)),
            dma((2, PARTS)),
            dma((2, PARTS)),
            dma((3,)),
            dma((3,)),
        ],
        compiler_params=pltpu.CompilerParams(
            collective_id=0, has_side_effects=True, vmem_limit_bytes=40 * 2**20
        ),
    )(*[pltpu.with_memory_space_constraint(a, pltpu.HBM) for a in args[:9]], args[9])
    return pl.pallas_call(
        update,
        name="adam_blend",
        out_shape=(
            jax.ShapeDtypeStruct((1, FEAT, COLS), BF16),
            jax.ShapeDtypeStruct((FEAT, COLS), F32),
        ),
        in_specs=[vmem] * 8,
        out_specs=(any_space, any_space),
        scratch_shapes=[pltpu.VMEM((FEAT, COLS), BF16), dma((PARTS,)), dma],
        compiler_params=pltpu.CompilerParams(vmem_limit_bytes=16 * 2**20),
    )(*parts)


def solution(mesh):
    placed = (
        P("rep", "fsdp", None),
        P("rep", "fsdp", None),
        P("rep", "fsdp", None),
        P("fsdp", None),
        P("fsdp", None),
        P("rep", "fsdp", None),
        P("rep", "fsdp", None),
        P("fsdp"),
        P(),
        P("rep"),
    )
    return jax.shard_map(
        local,
        mesh=mesh,
        in_specs=placed,
        out_specs=(P("rep", "fsdp", None), P("fsdp", None)),
        check_vma=False,
    )
```

```python
import functools

import jax
import jax.numpy as jnp
from jax import lax
from jax.experimental import pallas as pl
from jax.experimental.pallas import tpu as pltpu
from jax.sharding import PartitionSpec as P

HD = 128
ROWS = 8
EPS_NORM = 1e-06
BETA_ONE = 0.9
BETA_TWO = 0.999
ADAM_EPS = 1e-08
LEARN_RATE = 0.3
DECAY = 0.1
CLIP = 0.05
MOMENT_COEF = 0.9
OUTER_RATE = 0.7

MESH = pl.DeviceIdType.MESH
F32 = jnp.float32
BF16 = jnp.bfloat16

NY = 4
NZ = 8
REPS = 64
TOK = 384
FEAT = 1024
COLS = 512
HALF = 256
PARTS = 4
PROWS = FEAT // PARTS
YROWS = FEAT // NY
ZROWS = YROWS // NZ
NEAR = (1, 7, 2, 6, 3, 5, 4)


def place(x_lo, z, y, f):
    return (x_lo * (NZ * NY) + z * NY + y, f)


def kernel(
    weight,
    adam_first,
    adam_second,
    anchor,
    momentum,
    tokens,
    cotangent,
    plan_in,
    mix_weights_in,
    mix_index,
    linear,
    square,
    total_squares,
    level,
    moved_out,
    rate,
    kept_first,
    kept_second,
    plan,
    mix_weights,
    wown,
    wrecv,
    tch,
    tt,
    begun,
    cot,
    mask,
    picked,
    yrecv,
    ysum,
    zrecv,
    zsum,
    xrecv,
    mean,
    psend,
    precv,
    dch,
    gsend,
    grecv,
    gown,
    first,
    second,
    base,
    old,
    sq,
    ready_sem,
    small_sem,
    load_sem,
    wsend_sem,
    wrecv_sem,
    tsend_sem,
    trecv_sem,
    ysend_sem,
    yrecv_sem,
    zsend_sem,
    zrecv_sem,
    xsend_sem,
    xrecv_sem,
    azsend_sem,
    azrecv_sem,
    aysend_sem,
    ayrecv_sem,
    psend_sem,
    precv_sem,
    dsend_sem,
    drecv_sem,
    gsend_sem,
    grecv_sem,
    qsend_sem,
    qrecv_sem,
):
    rep = lax.axis_index("rep")
    f = lax.axis_index("fsdp")
    x_lo = rep // (NZ * NY)
    z = (rep // NY) % NZ
    y = rep % NY
    core = f % 2
    mate_f = f + 1 - 2 * core
    across_f = (f + 2) % 4
    diag_f = 3 - f
    mate = (rep, mate_f)
    across = (rep, across_f)
    diag = (rep, diag_f)
    y_peers = [place(x_lo, z, (y + d) % NY, f) for d in range(1, NY)]
    z_peers = [place(x_lo, (z + d) % NZ, y, f) for d in range(1, NZ)]
    x_peer = place(1 - x_lo, z, y, f)

    barrier = pltpu.get_barrier_semaphore()
    pl.semaphore_signal(barrier, inc=1, device_id=across, device_id_type=MESH)

    @pl.when(core == 1)
    def _():
        for peer in (mate, diag):
            pl.semaphore_signal(barrier, inc=1, device_id=peer, device_id_type=MESH)

    for d in range(1, NY):

        @pl.when((y + d) % NY > y)
        def _(peer=y_peers[d - 1]):
            pl.semaphore_signal(barrier, inc=1, device_id=peer, device_id_type=MESH)

    for d in range(1, NZ):

        @pl.when((z + d) % NZ > z)
        def _(peer=z_peers[d - 1]):
            pl.semaphore_signal(barrier, inc=1, device_id=peer, device_id_type=MESH)

    @pl.when(x_lo == 0)
    def _():
        pl.semaphore_signal(barrier, inc=1, device_id=x_peer, device_id_type=MESH)


    def columns(index):
        return pl.ds(pl.multiple_of(index * FEAT, FEAT), FEAT)

    pl.semaphore_wait(barrier, 3 - 2 * core + x_lo + y + z)

    def remote(src, dst, send, recv, to):
        return pltpu.make_async_remote_copy(
            src_ref=src, dst_ref=dst, send_sem=send, recv_sem=recv, device_id=to, device_id_type=MESH
        )

    w_copies = [
        remote(
            weight.at[0, :, pl.ds(j * HALF, HALF)], wrecv.at[j], wsend_sem.at[j], wrecv_sem.at[j], across
        )
        for j in range(2)
    ]
    for copy in w_copies:
        copy.start()
    small = [
        pltpu.make_async_copy(plan_in, plan, small_sem.at[0]),
        pltpu.make_async_copy(mix_weights_in, mix_weights, small_sem.at[1]),
    ]
    for copy in small:
        copy.start()
    loads = [
        pltpu.make_async_copy(weight.at[0], wown, load_sem.at[0]),
        pltpu.make_async_copy(
            tokens.at[0, :, columns(f)], tch.at[0, :, pl.ds(0, FEAT)], load_sem.at[1]
        ),
        pltpu.make_async_copy(
            tokens.at[0, :, columns(across_f)], tch.at[0, :, pl.ds(FEAT, FEAT)], load_sem.at[2]
        ),
        pltpu.make_async_copy(cotangent.at[0], cot, load_sem.at[3]),
        pltpu.make_async_copy(anchor, base, load_sem.at[4]),
        pltpu.make_async_copy(momentum, old, load_sem.at[5]),
        pltpu.make_async_copy(adam_first.at[0], first, load_sem.at[6]),
        pltpu.make_async_copy(adam_second.at[0], second, load_sem.at[7]),
    ]
    for copy in loads:
        copy.start()

    t_copies = [
        remote(
            tokens.at[0, :, columns(index)],
            tch.at[1, :, pl.ds(b * FEAT, FEAT)],
            tsend_sem.at[b],
            trecv_sem.at[b],
            mate,
        )
        for b, index in enumerate((mate_f, diag_f))
    ]
    @pl.when(core == 0)
    def _():
        for peer in (mate, diag):
            pl.semaphore_signal(ready_sem.at[2], inc=1, device_id=peer, device_id_type=MESH)

    for d in range(1, NZ):

        @pl.when((z + d) % NZ < z)
        def _(peer=z_peers[d - 1]):
            pl.semaphore_signal(ready_sem.at[1], inc=1, device_id=peer, device_id_type=MESH)

    @pl.when(x_lo == 1)
    def _():
        pl.semaphore_signal(ready_sem.at[1], inc=1, device_id=x_peer, device_id_type=MESH)

    for d in range(1, NY):

        @pl.when((y + d) % NY < y)
        def _(peer=y_peers[d - 1]):
            pl.semaphore_signal(ready_sem.at[0], inc=1, device_id=peer, device_id_type=MESH)


    for copy in small:
        copy.wait()

    def mark(i, _):
        mask[pl.ds(pl.multiple_of(i * ROWS, ROWS), ROWS), :] = jnp.full((ROWS, HD), plan[i], jnp.int32)
        return 0

    lax.fori_loop(0, FEAT // ROWS, mark, 0, unroll=8)

    loads[0].wait()

    def pick(start):
        def body(i, _):
            rows = pl.ds(pl.multiple_of(start + i * 32, 32), 32)
            chosen = mask[rows, :] == 0
            for k in range(HALF // HD):
                low = wown[rows, k * HD : (k + 1) * HD].astype(F32)
                high = wown[rows, HALF + k * HD : HALF + (k + 1) * HD].astype(F32)
                picked[rows, k * HD : (k + 1) * HD] = jnp.where(chosen, low, high).astype(BF16)
            return 0

        lax.fori_loop(0, YROWS // 64, body, 0, unroll=2)

    y_copies = [[], []]
    for part in range(2):
        for d in range(1, NY):
            start = ((y + d) % NY) * YROWS + part * (YROWS // 2)
            pick(start)
            if part == 0 and d == 1:

                @pl.when(y < NY - 1)
                def _():
                    pl.semaphore_wait(ready_sem.at[0], NY - 1 - y)

            copy = remote(
                picked.at[pl.ds(pl.multiple_of(start, YROWS // 2), YROWS // 2)],
                yrecv.at[d - 1, pl.ds(part * (YROWS // 2), YROWS // 2)],
                ysend_sem.at[d - 1, part],
                yrecv_sem.at[d - 1, part],
                y_peers[d - 1],
            )
            copy.start()
            y_copies[part].append(copy)
        pick(y * YROWS + part * (YROWS // 2))

    @pl.when(core == 1)
    def _():
        pl.semaphore_wait(ready_sem.at[2], 2)

    for copy in t_copies:
        copy.start()

    def turn(t):
        def body(i, _):
            at = pl.multiple_of(i * HD, HD)
            tt[pl.ds(at, HD), t * TOK : (t + 1) * TOK] = tch[t, :, pl.ds(at, HD)].T
            return 0

        lax.fori_loop(0, 2 * FEAT // HD, body, 0)

    loads[1].wait()
    loads[2].wait()
    turn(0)

    for copy in t_copies:
        copy.wait_recv()
    turn(1)
    def add_y(i, _):
        at = pl.multiple_of(i * 32, 32)
        rows = pl.ds(at, 32)
        total = picked[pl.ds(pl.multiple_of(y * YROWS + i * 32, 32), 32), :].astype(F32)
        for d in range(NY - 1):
            total = total + yrecv[d, rows, :].astype(F32)
        ysum[rows, :] = total
        return 0

    z_copies = []
    for d in range(1, NZ):
        start = pl.multiple_of(((z + d) % NZ) * ZROWS, ZROWS)
        z_copies.append(
            remote(
                ysum.at[pl.ds(start, ZROWS)],
                zrecv.at[d - 1],
                zsend_sem.at[d - 1],
                zrecv_sem.at[d - 1],
                z_peers[d - 1],
            )
        )
    for part in range(2):
        for copy in y_copies[part]:
            copy.wait_recv()
        lax.fori_loop(part * NZ // 2, (part + 1) * NZ // 2, add_y, 0)
        if part == 0:

            @pl.when(z + x_lo < NZ)
            def _():
                pl.semaphore_wait(ready_sem.at[1], NZ - z - x_lo)

        for d in range(1, NZ):
            pl.when(((z + d) % NZ) // (NZ // 2) == part)(z_copies[d - 1].start)

    loads[3].wait()

    own_block = pl.ds(0, FEAT)
    across_block = pl.ds(FEAT, FEAT)
    p_copies = []
    d_copies = []
    g_copies = []

    def prepare(t, j):
        begun[t, j] = jnp.dot(
            tch[t, :, own_block], wown[:, j * HALF : (j + 1) * HALF], preferred_element_type=F32
        )

    def project(t, j):
        return begun[t, j] + jnp.dot(tch[t, :, across_block], wrecv[j], preferred_element_type=F32)

    def add_z():
        for copy in z_copies:
            copy.wait_recv()
        total = ysum[pl.ds(pl.multiple_of(z * ZROWS, ZROWS), ZROWS), :]
        for d in range(NZ - 1):
            total = total + zrecv[d]
        zsum[...] = total
        x_copy.start()

    def slice_of(d):
        start = y * YROWS + ((z + NZ - d) % NZ) * ZROWS
        return pl.ds(pl.multiple_of(start, ZROWS), ZROWS)

    def spread(d):
        rows = slice_of(d)
        for e in range(NY - 1):
            copy = remote(
                mean.at[rows], mean.at[rows], aysend_sem.at[d, e], ayrecv_sem.at[d, e], y_peers[e]
            )
            copy.start()
            ay_copies.append(copy)

    def add_x():
        x_copy.wait_recv()
        rows = slice_of(0)
        mean[rows, :] = (zsum[...] + xrecv[...]) * (1.0 / REPS)
        for d in NEAR:
            az_copies[d] = remote(
                mean.at[rows], mean.at[rows], azsend_sem.at[d - 1], azrecv_sem.at[d - 1], z_peers[d - 1]
            )
            az_copies[d].start()
        spread(0)

    def forward(*steps):
        for d in steps:
            az_copies[d].wait_recv()
            spread(d)

    x_copy = remote(zsum, xrecv, xsend_sem, xrecv_sem, x_peer)
    az_copies = {}
    ay_copies = []

    def chunk(j):
        w_copies[j].wait_recv()
        psend[j] = project(1, j)
        p_copy = remote(psend.at[j], precv.at[j], psend_sem.at[j], precv_sem.at[j], mate)
        p_copy.start()
        p_copies.append(p_copy)
        keys = project(0, j)
        p_copy.wait_recv()
        keys = keys + precv[j]
        for k in range(HALF // HD):
            at = j * HALF + k * HD
            head = keys[:, k * HD : (k + 1) * HD]
            pull = cot[:, at : at + HD].astype(F32)
            scale = lax.rsqrt(jnp.sum(head * head, axis=1, keepdims=True) * (1.0 / HD) + EPS_NORM)
            inner = jnp.sum(head * pull, axis=1, keepdims=True) * (1.0 / HD)
            back = scale * (pull - head * (scale * scale * inner))
            dch[j, 0, :, k * HD : (k + 1) * HD] = back.astype(BF16)
        d_copy = remote(dch.at[j, 0], dch.at[j, 1], dsend_sem.at[j], drecv_sem.at[j], mate)
        d_copy.start()
        d_copies.append(d_copy)
        if j == 0:
            add_z()
        d_copy.wait_recv()

        def grad(at):
            low = jnp.dot(tt[pl.ds(at, PROWS), 0:TOK], dch[j, 0], preferred_element_type=F32)
            high = jnp.dot(
                tt[pl.ds(at, PROWS), TOK : 2 * TOK], dch[j, 1], preferred_element_type=F32
            )
            return low + high

        for i in range(PARTS):
            gsend[j, i] = grad(FEAT + i * PROWS).astype(BF16)
            g_copy = remote(
                gsend.at[j, i], grecv.at[j, i], gsend_sem.at[j, i], grecv_sem.at[j, i], across
            )
            g_copy.start()
            g_copies.append(g_copy)
        for i in range(PARTS):
            gown[j, i] = grad(i * PROWS)

    for t in range(2):
        for j in range(2):
            prepare(t, j)

    chunk(0)
    add_x()
    chunk(1)
    forward(*NEAR)

    def gather(j, i, total):
        g_copies[j * PARTS + i].wait_recv()

        def body(s, total):
            rows = pl.ds(pl.multiple_of(s * 32, 32), 32)
            grad = (gown[j, i, rows, :] + grecv[j, i, rows, :].astype(F32)) * (1.0 / (4 * TOK))
            linear[j, i, rows, :] = (1.0 - BETA_ONE) * grad
            power = grad * grad
            square[j, i, rows, :] = (1.0 - BETA_TWO) * power
            for r in range(4):
                for k in range(HALF // HD):
                    total = total + power[r * 8 : (r + 1) * 8, k * HD : (k + 1) * HD]
            return total

        return lax.fori_loop(0, PROWS // 32, body, total, unroll=2)

    squares = jnp.zeros((8, HD), F32)
    for i in range(PARTS):
        squares = gather(0, i, squares)

    for copy in loads[4:]:
        copy.wait()

    def decay(i, _):
        rows = pl.ds(pl.multiple_of(i * 16, 16), 16)
        kept_first[rows, :] = BETA_ONE * first[rows, :].astype(F32)
        kept_second[rows, :] = BETA_TWO * second[rows, :].astype(F32)
        return 0

    lax.fori_loop(0, FEAT // 16, decay, 0)
    choice = mix_index[0]
    alpha = mix_weights[0]
    for k in range(1, 4):
        alpha = jnp.where(choice == k, mix_weights[k], alpha)
    for copy in ay_copies:
        copy.wait_recv()

    def outer_step(i, _):
        rows = pl.ds(pl.multiple_of(i * 16, 16), 16)
        row_frag = mask[rows, :]
        for index in range(2):
            rate[index, rows, :] = jnp.where(row_frag == index, alpha * LEARN_RATE, LEARN_RATE)
        for k in range(HALF // HD):
            middle = mean[rows, k * HD : (k + 1) * HD]
            for index in range(2):
                at = index * HALF + k * HD
                chosen = row_frag == index
                start = base[rows, at : at + HD].astype(F32)
                wide = wown[rows, at : at + HD].astype(F32) * (1.0 - LEARN_RATE * DECAY)
                before = old[rows, at : at + HD]
                average = start - middle
                moved = MOMENT_COEF * before + average
                outer = start - OUTER_RATE * (average + MOMENT_COEF * moved)
                moved_out[rows, at : at + HD] = jnp.where(chosen, moved, before)
                level[rows, at : at + HD] = jnp.where(
                    chosen, alpha * wide + (1.0 - alpha) * outer, wide
                )
        return 0

    lax.fori_loop(0, FEAT // 16, outer_step, 0)

    for i in range(PARTS):
        squares = gather(1, i, squares)
    sq[0] = squares
    q_copies = []
    for d, peer in enumerate((mate, across, diag)):
        q_copies.append(remote(sq.at[0], sq.at[1 + d], qsend_sem.at[d], qrecv_sem.at[d], peer))
        q_copies[-1].start()
    for copy in q_copies:
        copy.wait_recv()
    total_squares[...] = sq[0] + sq[1] + sq[2] + sq[3]

    sent = w_copies + t_copies + y_copies[0] + y_copies[1] + z_copies + [x_copy] + list(az_copies.values()) + ay_copies
    for copy in sent + p_copies + d_copies + g_copies + q_copies:
        copy.wait_send()


def update(
    linear,
    square,
    total_squares,
    level,
    moved,
    rate,
    kept_first,
    kept_second,
    new_weight,
    new_momentum,
    result,
    weight_sem,
    momentum_sem,
):
    momentum_copy = pltpu.make_async_copy(moved, new_momentum, momentum_sem)
    momentum_copy.start()
    everything = jnp.sum(total_squares[...], keepdims=True)
    clip = jnp.minimum(1.0, CLIP / jnp.sqrt(everything + 1e-12))
    ratio = jnp.broadcast_to(clip, (16, HD))
    ratio_squared = ratio * ratio
    copies = []
    for i in range(PARTS):

        def adam(s, _, i=i):
            at = pl.multiple_of(s * 16, 16)
            rows = pl.ds(pl.multiple_of(i * PROWS + s * 16, 16), 16)
            for j in range(2):
                speed = rate[j, rows, :]
                for k in range(HALF // HD):
                    c = j * HALF + k * HD
                    block = (j, i, pl.ds(at, 16), slice(k * HD, (k + 1) * HD))
                    one = kept_first[rows, c : c + HD] + linear[block] * ratio
                    two = kept_second[rows, c : c + HD] + square[block] * ratio_squared
                    step = one / (two * lax.rsqrt(two) + ADAM_EPS)
                    result[rows, c : c + HD] = (level[rows, c : c + HD] - speed * step).astype(BF16)
            return 0

        lax.fori_loop(0, PROWS // 16, adam, 0, unroll=4)
        block = pl.ds(i * PROWS, PROWS)
        copy = pltpu.make_async_copy(result.at[block], new_weight.at[0, block], weight_sem.at[i])
        copy.start()
        copies.append(copy)
    for copy in copies:
        copy.wait()
    momentum_copy.wait()


def local(*args):
    dma = pltpu.SemaphoreType.DMA
    any_space = pl.BlockSpec(memory_space=pl.ANY)
    vmem = pl.BlockSpec(memory_space=pltpu.VMEM)
    parts = pl.pallas_call(
        kernel,
        name="diloco_step",
        out_shape=(
            jax.ShapeDtypeStruct((2, PARTS, PROWS, HALF), F32),
            jax.ShapeDtypeStruct((2, PARTS, PROWS, HALF), F32),
            jax.ShapeDtypeStruct((8, HD), F32),
            jax.ShapeDtypeStruct((FEAT, COLS), F32),
            jax.ShapeDtypeStruct((FEAT, COLS), F32),
            jax.ShapeDtypeStruct((2, FEAT, HD), F32),
            jax.ShapeDtypeStruct((FEAT, COLS), F32),
            jax.ShapeDtypeStruct((FEAT, COLS), F32),
        ),
        in_specs=[any_space] * 9 + [pl.BlockSpec(memory_space=pltpu.SMEM)],
        out_specs=(vmem,) * 8,
        scratch_shapes=[
            pltpu.SMEM((FEAT // ROWS,), jnp.int32),
            pltpu.SMEM((4,), F32),
            pltpu.VMEM((FEAT, COLS), BF16),
            pltpu.VMEM((2, FEAT, HALF), BF16),
            pltpu.VMEM((2, TOK, 2 * FEAT), BF16),
            pltpu.VMEM((2 * FEAT, 2 * TOK), BF16),
            pltpu.VMEM((2, 2, TOK, HALF), F32),
            pltpu.VMEM((TOK, COLS), BF16),
            pltpu.VMEM((FEAT, HD), jnp.int32),
            pltpu.VMEM((FEAT, HALF), BF16),
            pltpu.VMEM((NY - 1, YROWS, HALF), BF16),
            pltpu.VMEM((YROWS, HALF), F32),
            pltpu.VMEM((NZ - 1, ZROWS, HALF), F32),
            pltpu.VMEM((ZROWS, HALF), F32),
            pltpu.VMEM((ZROWS, HALF), F32),
            pltpu.VMEM((FEAT, HALF), F32),
            pltpu.VMEM((2, TOK, HALF), F32),
            pltpu.VMEM((2, TOK, HALF), F32),
            pltpu.VMEM((2, 2, TOK, HALF), BF16),
            pltpu.VMEM((2, PARTS, PROWS, HALF), BF16),
            pltpu.VMEM((2, PARTS, PROWS, HALF), BF16),
            pltpu.VMEM((2, PARTS, PROWS, HALF), F32),
            pltpu.VMEM((FEAT, COLS), BF16),
            pltpu.VMEM((FEAT, COLS), BF16),
            pltpu.VMEM((FEAT, COLS), BF16),
            pltpu.VMEM((FEAT, COLS), F32),
            pltpu.VMEM((4, 8, HD), F32),
            pltpu.SemaphoreType.REGULAR((3,)),
            dma((2,)),
            dma((8,)),
            dma((2,)),
            dma((2,)),
            dma((2,)),
            dma((2,)),
            dma((NY - 1, 2)),
            dma((NY - 1, 2)),
            dma((NZ - 1,)),
            dma((NZ - 1,)),
            dma,
            dma,
            dma((NZ - 1,)),
            dma((NZ - 1,)),
            dma((NZ, NY - 1)),
            dma((NZ, NY - 1)),
            dma((2,)),
            dma((2,)),
            dma((2,)),
            dma((2,)),
            dma((2, PARTS)),
            dma((2, PARTS)),
            dma((3,)),
            dma((3,)),
        ],
        compiler_params=pltpu.CompilerParams(
            collective_id=0, has_side_effects=True, vmem_limit_bytes=40 * 2**20
        ),
    )(*[pltpu.with_memory_space_constraint(a, pltpu.HBM) for a in args[:9]], args[9])
    return pl.pallas_call(
        update,
        name="adam_blend",
        out_shape=(
            jax.ShapeDtypeStruct((1, FEAT, COLS), BF16),
            jax.ShapeDtypeStruct((FEAT, COLS), F32),
        ),
        in_specs=[vmem] * 8,
        out_specs=(any_space, any_space),
        scratch_shapes=[pltpu.VMEM((FEAT, COLS), BF16), dma((PARTS,)), dma],
        compiler_params=pltpu.CompilerParams(vmem_limit_bytes=16 * 2**20),
    )(*parts)


def solution(mesh):
    placed = (
        P("rep", "fsdp", None),
        P("rep", "fsdp", None),
        P("rep", "fsdp", None),
        P("fsdp", None),
        P("fsdp", None),
        P("rep", "fsdp", None),
        P("rep", "fsdp", None),
        P("fsdp"),
        P(),
        P("rep"),
    )
    return jax.shard_map(
        local,
        mesh=mesh,
        in_specs=placed,
        out_specs=(P("rep", "fsdp", None), P("fsdp", None)),
        check_vma=False,
    )
```

```python
import functools

import jax
import jax.numpy as jnp
from jax import lax
from jax.experimental import pallas as pl
from jax.experimental.pallas import tpu as pltpu
from jax.sharding import PartitionSpec as P

HD = 128
ROWS = 8
EPS_NORM = 1e-06
BETA_ONE = 0.9
BETA_TWO = 0.999
ADAM_EPS = 1e-08
LEARN_RATE = 0.3
DECAY = 0.1
CLIP = 0.05
MOMENT_COEF = 0.9
OUTER_RATE = 0.7

MESH = pl.DeviceIdType.MESH
F32 = jnp.float32
BF16 = jnp.bfloat16

NY = 4
NZ = 8
REPS = 64
TOK = 384
FEAT = 1024
COLS = 512
HALF = 256
PARTS = 4
PROWS = FEAT // PARTS
YROWS = FEAT // NY
ZROWS = YROWS // NZ
NEAR = (1, 7, 2, 6, 3, 5, 4)


def place(x_lo, z, y, f):
    return (x_lo * (NZ * NY) + z * NY + y, f)


def kernel(
    weight,
    adam_first,
    adam_second,
    anchor,
    momentum,
    tokens,
    cotangent,
    plan_in,
    mix_weights_in,
    mix_index,
    linear,
    square,
    total_squares,
    level,
    moved_out,
    rate,
    kept_first,
    kept_second,
    plan,
    mix_weights,
    wown,
    wrecv,
    tch,
    tt,
    begun,
    cot,
    mask,
    picked,
    yrecv,
    ysum,
    zrecv,
    zsum,
    xrecv,
    mean,
    psend,
    precv,
    dch,
    gsend,
    grecv,
    gown,
    first,
    second,
    base,
    old,
    sq,
    ready_sem,
    small_sem,
    load_sem,
    wsend_sem,
    wrecv_sem,
    tsend_sem,
    trecv_sem,
    ysend_sem,
    yrecv_sem,
    zsend_sem,
    zrecv_sem,
    xsend_sem,
    xrecv_sem,
    azsend_sem,
    azrecv_sem,
    aysend_sem,
    ayrecv_sem,
    psend_sem,
    precv_sem,
    dsend_sem,
    drecv_sem,
    gsend_sem,
    grecv_sem,
    qsend_sem,
    qrecv_sem,
):
    rep = lax.axis_index("rep")
    f = lax.axis_index("fsdp")
    x_lo = rep // (NZ * NY)
    z = (rep // NY) % NZ
    y = rep % NY
    core = f % 2
    mate_f = f + 1 - 2 * core
    across_f = (f + 2) % 4
    diag_f = 3 - f
    mate = (rep, mate_f)
    across = (rep, across_f)
    diag = (rep, diag_f)
    y_peers = [place(x_lo, z, (y + d) % NY, f) for d in range(1, NY)]
    z_peers = [place(x_lo, (z + d) % NZ, y, f) for d in range(1, NZ)]
    x_peer = place(1 - x_lo, z, y, f)

    barrier = pltpu.get_barrier_semaphore()
    pl.semaphore_signal(barrier, inc=1, device_id=across, device_id_type=MESH)

    @pl.when(core == 1)
    def _():
        for peer in (mate, diag):
            pl.semaphore_signal(barrier, inc=1, device_id=peer, device_id_type=MESH)

    for d in range(1, NY):

        @pl.when((y + d) % NY > y)
        def _(peer=y_peers[d - 1]):
            pl.semaphore_signal(barrier, inc=1, device_id=peer, device_id_type=MESH)

    for d in range(1, NZ):

        @pl.when((z + d) % NZ > z)
        def _(peer=z_peers[d - 1]):
            pl.semaphore_signal(barrier, inc=1, device_id=peer, device_id_type=MESH)

    @pl.when(x_lo == 0)
    def _():
        pl.semaphore_signal(barrier, inc=1, device_id=x_peer, device_id_type=MESH)


    def columns(index):
        return pl.ds(pl.multiple_of(index * FEAT, FEAT), FEAT)

    pl.semaphore_wait(barrier, 3 - 2 * core + x_lo + y + z)

    def remote(src, dst, send, recv, to):
        return pltpu.make_async_remote_copy(
            src_ref=src, dst_ref=dst, send_sem=send, recv_sem=recv, device_id=to, device_id_type=MESH
        )

    w_copies = [
        remote(
            weight.at[0, :, pl.ds(j * HALF, HALF)], wrecv.at[j], wsend_sem.at[j], wrecv_sem.at[j], across
        )
        for j in range(2)
    ]
    for copy in w_copies:
        copy.start()
    small = [
        pltpu.make_async_copy(plan_in, plan, small_sem.at[0]),
        pltpu.make_async_copy(mix_weights_in, mix_weights, small_sem.at[1]),
    ]
    for copy in small:
        copy.start()
    loads = [
        pltpu.make_async_copy(weight.at[0], wown, load_sem.at[0]),
        pltpu.make_async_copy(
            tokens.at[0, :, columns(f)], tch.at[0, :, pl.ds(0, FEAT)], load_sem.at[1]
        ),
        pltpu.make_async_copy(
            tokens.at[0, :, columns(across_f)], tch.at[0, :, pl.ds(FEAT, FEAT)], load_sem.at[2]
        ),
        pltpu.make_async_copy(cotangent.at[0], cot, load_sem.at[3]),
        pltpu.make_async_copy(anchor, base, load_sem.at[4]),
        pltpu.make_async_copy(momentum, old, load_sem.at[5]),
        pltpu.make_async_copy(adam_first.at[0], first, load_sem.at[6]),
        pltpu.make_async_copy(adam_second.at[0], second, load_sem.at[7]),
    ]
    for copy in loads:
        copy.start()

    t_copies = [
        remote(
            tokens.at[0, :, columns(index)],
            tch.at[1, :, pl.ds(b * FEAT, FEAT)],
            tsend_sem.at[b],
            trecv_sem.at[b],
            mate,
        )
        for b, index in enumerate((mate_f, diag_f))
    ]
    @pl.when(core == 0)
    def _():
        for peer in (mate, diag):
            pl.semaphore_signal(ready_sem.at[2], inc=1, device_id=peer, device_id_type=MESH)

    for d in range(1, NZ):

        @pl.when((z + d) % NZ < z)
        def _(peer=z_peers[d - 1]):
            pl.semaphore_signal(ready_sem.at[1], inc=1, device_id=peer, device_id_type=MESH)

    @pl.when(x_lo == 1)
    def _():
        pl.semaphore_signal(ready_sem.at[1], inc=1, device_id=x_peer, device_id_type=MESH)

    for d in range(1, NY):

        @pl.when((y + d) % NY < y)
        def _(peer=y_peers[d - 1]):
            pl.semaphore_signal(ready_sem.at[0], inc=1, device_id=peer, device_id_type=MESH)


    for copy in small:
        copy.wait()

    def mark(i, _):
        mask[pl.ds(pl.multiple_of(i * ROWS, ROWS), ROWS), :] = jnp.full((ROWS, HD), plan[i], jnp.int32)
        return 0

    lax.fori_loop(0, FEAT // ROWS, mark, 0, unroll=8)

    loads[0].wait()

    def pick(start):
        def body(i, _):
            rows = pl.ds(pl.multiple_of(start + i * 32, 32), 32)
            chosen = mask[rows, :] == 0
            for k in range(HALF // HD):
                low = wown[rows, k * HD : (k + 1) * HD].astype(F32)
                high = wown[rows, HALF + k * HD : HALF + (k + 1) * HD].astype(F32)
                picked[rows, k * HD : (k + 1) * HD] = jnp.where(chosen, low, high).astype(BF16)
            return 0

        lax.fori_loop(0, YROWS // 64, body, 0, unroll=2)

    y_copies = [[], []]
    for part in range(2):
        for d in range(1, NY):
            start = ((y + d) % NY) * YROWS + part * (YROWS // 2)
            pick(start)
            if part == 0 and d == 1:

                @pl.when(y < NY - 1)
                def _():
                    pl.semaphore_wait(ready_sem.at[0], NY - 1 - y)

            copy = remote(
                picked.at[pl.ds(pl.multiple_of(start, YROWS // 2), YROWS // 2)],
                yrecv.at[d - 1, pl.ds(part * (YROWS // 2), YROWS // 2)],
                ysend_sem.at[d - 1, part],
                yrecv_sem.at[d - 1, part],
                y_peers[d - 1],
            )
            copy.start()
            y_copies[part].append(copy)
        pick(y * YROWS + part * (YROWS // 2))

    @pl.when(core == 1)
    def _():
        pl.semaphore_wait(ready_sem.at[2], 2)

    for copy in t_copies:
        copy.start()

    def turn(t):
        def body(i, _):
            at = pl.multiple_of(i * HD, HD)
            tt[pl.ds(at, HD), t * TOK : (t + 1) * TOK] = tch[t, :, pl.ds(at, HD)].T
            return 0

        lax.fori_loop(0, 2 * FEAT // HD, body, 0)

    loads[1].wait()
    loads[2].wait()
    turn(0)

    for copy in t_copies:
        copy.wait_recv()
    turn(1)
    def add_y(i, _):
        at = pl.multiple_of(i * 32, 32)
        rows = pl.ds(at, 32)
        total = picked[pl.ds(pl.multiple_of(y * YROWS + i * 32, 32), 32), :].astype(F32)
        for d in range(NY - 1):
            total = total + yrecv[d, rows, :].astype(F32)
        ysum[rows, :] = total
        return 0

    z_copies = []
    for d in range(1, NZ):
        start = pl.multiple_of(((z + d) % NZ) * ZROWS, ZROWS)
        z_copies.append(
            remote(
                ysum.at[pl.ds(start, ZROWS)],
                zrecv.at[d - 1],
                zsend_sem.at[d - 1],
                zrecv_sem.at[d - 1],
                z_peers[d - 1],
            )
        )
    for part in range(2):
        for copy in y_copies[part]:
            copy.wait_recv()
        lax.fori_loop(part * NZ // 2, (part + 1) * NZ // 2, add_y, 0)
        if part == 0:

            @pl.when(z + x_lo < NZ)
            def _():
                pl.semaphore_wait(ready_sem.at[1], NZ - z - x_lo)

        for d in range(1, NZ):
            pl.when(((z + d) % NZ) // (NZ // 2) == part)(z_copies[d - 1].start)

    loads[3].wait()

    own_block = pl.ds(0, FEAT)
    across_block = pl.ds(FEAT, FEAT)
    p_copies = []
    d_copies = []
    g_copies = []

    def prepare(t, j):
        begun[t, j] = jnp.dot(
            tch[t, :, own_block], wown[:, j * HALF : (j + 1) * HALF], preferred_element_type=F32
        )

    def project(t, j):
        return begun[t, j] + jnp.dot(tch[t, :, across_block], wrecv[j], preferred_element_type=F32)

    def add_z():
        for copy in z_copies:
            copy.wait_recv()
        total = ysum[pl.ds(pl.multiple_of(z * ZROWS, ZROWS), ZROWS), :]
        for d in range(NZ - 1):
            total = total + zrecv[d]
        zsum[...] = total
        x_copy.start()

    def slice_of(d):
        start = y * YROWS + ((z + NZ - d) % NZ) * ZROWS
        return pl.ds(pl.multiple_of(start, ZROWS), ZROWS)

    def spread(d):
        rows = slice_of(d)
        for e in range(NY - 1):
            copy = remote(
                mean.at[rows], mean.at[rows], aysend_sem.at[d, e], ayrecv_sem.at[d, e], y_peers[e]
            )
            copy.start()
            ay_copies.append(copy)

    def add_x():
        x_copy.wait_recv()
        rows = slice_of(0)
        mean[rows, :] = (zsum[...] + xrecv[...]) * (1.0 / REPS)
        for d in NEAR:
            az_copies[d] = remote(
                mean.at[rows], mean.at[rows], azsend_sem.at[d - 1], azrecv_sem.at[d - 1], z_peers[d - 1]
            )
            az_copies[d].start()
        spread(0)

    def forward(*steps):
        for d in steps:
            az_copies[d].wait_recv()
            spread(d)

    x_copy = remote(zsum, xrecv, xsend_sem, xrecv_sem, x_peer)
    az_copies = {}
    ay_copies = []

    def chunk(j):
        w_copies[j].wait_recv()
        psend[j] = project(1, j)
        p_copy = remote(psend.at[j], precv.at[j], psend_sem.at[j], precv_sem.at[j], mate)
        p_copy.start()
        p_copies.append(p_copy)
        keys = project(0, j)
        p_copy.wait_recv()
        keys = keys + precv[j]
        for k in range(HALF // HD):
            at = j * HALF + k * HD
            head = keys[:, k * HD : (k + 1) * HD]
            pull = cot[:, at : at + HD].astype(F32)
            scale = lax.rsqrt(jnp.sum(head * head, axis=1, keepdims=True) * (1.0 / HD) + EPS_NORM)
            inner = jnp.sum(head * pull, axis=1, keepdims=True) * (1.0 / HD)
            back = scale * (pull - head * (scale * scale * inner))
            dch[j, 0, :, k * HD : (k + 1) * HD] = back.astype(BF16)
        d_copy = remote(dch.at[j, 0], dch.at[j, 1], dsend_sem.at[j], drecv_sem.at[j], mate)
        d_copy.start()
        d_copies.append(d_copy)
        if j == 0:
            add_z()
        d_copy.wait_recv()

        def grad(at):
            low = jnp.dot(tt[pl.ds(at, PROWS), 0:TOK], dch[j, 0], preferred_element_type=F32)
            high = jnp.dot(
                tt[pl.ds(at, PROWS), TOK : 2 * TOK], dch[j, 1], preferred_element_type=F32
            )
            return low + high

        for i in range(PARTS):
            gsend[j, i] = grad(FEAT + i * PROWS).astype(BF16)
            g_copy = remote(
                gsend.at[j, i], grecv.at[j, i], gsend_sem.at[j, i], grecv_sem.at[j, i], across
            )
            g_copy.start()
            g_copies.append(g_copy)
        for i in range(PARTS):
            gown[j, i] = grad(i * PROWS)

    for t in range(2):
        for j in range(2):
            prepare(t, j)

    chunk(0)
    add_x()
    chunk(1)
    forward(*NEAR)

    def gather(j, i, total):
        g_copies[j * PARTS + i].wait_recv()

        def body(s, total):
            rows = pl.ds(pl.multiple_of(s * 32, 32), 32)
            grad = (gown[j, i, rows, :] + grecv[j, i, rows, :].astype(F32)) * (1.0 / (4 * TOK))
            linear[j, i, rows, :] = (1.0 - BETA_ONE) * grad
            power = grad * grad
            square[j, i, rows, :] = (1.0 - BETA_TWO) * power
            for r in range(4):
                for k in range(HALF // HD):
                    total = total + power[r * 8 : (r + 1) * 8, k * HD : (k + 1) * HD]
            return total

        return lax.fori_loop(0, PROWS // 32, body, total, unroll=2)

    squares = jnp.zeros((8, HD), F32)
    for i in range(PARTS):
        squares = gather(0, i, squares)

    for copy in loads[4:]:
        copy.wait()

    def decay(i, _):
        rows = pl.ds(pl.multiple_of(i * 16, 16), 16)
        kept_first[rows, :] = BETA_ONE * first[rows, :].astype(F32)
        kept_second[rows, :] = BETA_TWO * second[rows, :].astype(F32)
        return 0

    lax.fori_loop(0, FEAT // 16, decay, 0)
    choice = mix_index[0]
    alpha = mix_weights[0]
    for k in range(1, 4):
        alpha = jnp.where(choice == k, mix_weights[k], alpha)
    for copy in ay_copies:
        copy.wait_recv()

    def outer_step(i, _):
        rows = pl.ds(pl.multiple_of(i * 16, 16), 16)
        row_frag = mask[rows, :]
        for index in range(2):
            rate[index, rows, :] = jnp.where(row_frag == index, alpha * LEARN_RATE, LEARN_RATE)
        for k in range(HALF // HD):
            middle = mean[rows, k * HD : (k + 1) * HD]
            for index in range(2):
                at = index * HALF + k * HD
                chosen = row_frag == index
                start = base[rows, at : at + HD].astype(F32)
                wide = wown[rows, at : at + HD].astype(F32) * (1.0 - LEARN_RATE * DECAY)
                before = old[rows, at : at + HD]
                average = start - middle
                moved = MOMENT_COEF * before + average
                outer = start - OUTER_RATE * (average + MOMENT_COEF * moved)
                moved_out[rows, at : at + HD] = jnp.where(chosen, moved, before)
                level[rows, at : at + HD] = jnp.where(
                    chosen, alpha * wide + (1.0 - alpha) * outer, wide
                )
        return 0

    lax.fori_loop(0, FEAT // 16, outer_step, 0)

    for i in range(PARTS):
        squares = gather(1, i, squares)
    sq[0] = squares
    q_copies = []
    for d, peer in enumerate((mate, across, diag)):
        q_copies.append(remote(sq.at[0], sq.at[1 + d], qsend_sem.at[d], qrecv_sem.at[d], peer))
        q_copies[-1].start()
    for copy in q_copies:
        copy.wait_recv()
    total_squares[...] = sq[0] + sq[1] + sq[2] + sq[3]

    sent = w_copies + t_copies + y_copies[0] + y_copies[1] + z_copies + [x_copy] + list(az_copies.values()) + ay_copies
    for copy in sent + p_copies + d_copies + g_copies + q_copies:
        copy.wait_send()


def update(
    linear,
    square,
    total_squares,
    level,
    moved,
    rate,
    kept_first,
    kept_second,
    new_weight,
    new_momentum,
    result,
    weight_sem,
    momentum_sem,
):
    momentum_copy = pltpu.make_async_copy(moved, new_momentum, momentum_sem)
    momentum_copy.start()
    everything = jnp.sum(total_squares[...], keepdims=True)
    clip = jnp.minimum(1.0, CLIP / jnp.sqrt(everything + 1e-12))
    ratio = jnp.broadcast_to(clip, (16, HD))
    ratio_squared = ratio * ratio
    copies = []
    for i in range(PARTS):

        def adam(s, _, i=i):
            at = pl.multiple_of(s * 16, 16)
            rows = pl.ds(pl.multiple_of(i * PROWS + s * 16, 16), 16)
            for j in range(2):
                speed = rate[j, rows, :]
                for k in range(HALF // HD):
                    c = j * HALF + k * HD
                    block = (j, i, pl.ds(at, 16), slice(k * HD, (k + 1) * HD))
                    one = kept_first[rows, c : c + HD] + linear[block] * ratio
                    two = kept_second[rows, c : c + HD] + square[block] * ratio_squared
                    step = one / (two * lax.rsqrt(two) + ADAM_EPS)
                    result[rows, c : c + HD] = (level[rows, c : c + HD] - speed * step).astype(BF16)
            return 0

        for h in range(2):
            lax.fori_loop(h * (PROWS // 32), (h + 1) * (PROWS // 32), adam, 0, unroll=8)
            block = pl.ds(i * PROWS + h * (PROWS // 2), PROWS // 2)
            copy = pltpu.make_async_copy(
                result.at[block], new_weight.at[0, block], weight_sem.at[2 * i + h]
            )
            copy.start()
            copies.append(copy)
    for copy in copies:
        copy.wait()
    momentum_copy.wait()


def local(*args):
    dma = pltpu.SemaphoreType.DMA
    any_space = pl.BlockSpec(memory_space=pl.ANY)
    vmem = pl.BlockSpec(memory_space=pltpu.VMEM)
    parts = pl.pallas_call(
        kernel,
        name="diloco_step",
        out_shape=(
            jax.ShapeDtypeStruct((2, PARTS, PROWS, HALF), F32),
            jax.ShapeDtypeStruct((2, PARTS, PROWS, HALF), F32),
            jax.ShapeDtypeStruct((8, HD), F32),
            jax.ShapeDtypeStruct((FEAT, COLS), F32),
            jax.ShapeDtypeStruct((FEAT, COLS), F32),
            jax.ShapeDtypeStruct((2, FEAT, HD), F32),
            jax.ShapeDtypeStruct((FEAT, COLS), F32),
            jax.ShapeDtypeStruct((FEAT, COLS), F32),
        ),
        in_specs=[any_space] * 9 + [pl.BlockSpec(memory_space=pltpu.SMEM)],
        out_specs=(vmem,) * 8,
        scratch_shapes=[
            pltpu.SMEM((FEAT // ROWS,), jnp.int32),
            pltpu.SMEM((4,), F32),
            pltpu.VMEM((FEAT, COLS), BF16),
            pltpu.VMEM((2, FEAT, HALF), BF16),
            pltpu.VMEM((2, TOK, 2 * FEAT), BF16),
            pltpu.VMEM((2 * FEAT, 2 * TOK), BF16),
            pltpu.VMEM((2, 2, TOK, HALF), F32),
            pltpu.VMEM((TOK, COLS), BF16),
            pltpu.VMEM((FEAT, HD), jnp.int32),
            pltpu.VMEM((FEAT, HALF), BF16),
            pltpu.VMEM((NY - 1, YROWS, HALF), BF16),
            pltpu.VMEM((YROWS, HALF), F32),
            pltpu.VMEM((NZ - 1, ZROWS, HALF), F32),
            pltpu.VMEM((ZROWS, HALF), F32),
            pltpu.VMEM((ZROWS, HALF), F32),
            pltpu.VMEM((FEAT, HALF), F32),
            pltpu.VMEM((2, TOK, HALF), F32),
            pltpu.VMEM((2, TOK, HALF), F32),
            pltpu.VMEM((2, 2, TOK, HALF), BF16),
            pltpu.VMEM((2, PARTS, PROWS, HALF), BF16),
            pltpu.VMEM((2, PARTS, PROWS, HALF), BF16),
            pltpu.VMEM((2, PARTS, PROWS, HALF), F32),
            pltpu.VMEM((FEAT, COLS), BF16),
            pltpu.VMEM((FEAT, COLS), BF16),
            pltpu.VMEM((FEAT, COLS), BF16),
            pltpu.VMEM((FEAT, COLS), F32),
            pltpu.VMEM((4, 8, HD), F32),
            pltpu.SemaphoreType.REGULAR((3,)),
            dma((2,)),
            dma((8,)),
            dma((2,)),
            dma((2,)),
            dma((2,)),
            dma((2,)),
            dma((NY - 1, 2)),
            dma((NY - 1, 2)),
            dma((NZ - 1,)),
            dma((NZ - 1,)),
            dma,
            dma,
            dma((NZ - 1,)),
            dma((NZ - 1,)),
            dma((NZ, NY - 1)),
            dma((NZ, NY - 1)),
            dma((2,)),
            dma((2,)),
            dma((2,)),
            dma((2,)),
            dma((2, PARTS)),
            dma((2, PARTS)),
            dma((3,)),
            dma((3,)),
        ],
        compiler_params=pltpu.CompilerParams(
            collective_id=0, has_side_effects=True, vmem_limit_bytes=40 * 2**20
        ),
    )(*[pltpu.with_memory_space_constraint(a, pltpu.HBM) for a in args[:9]], args[9])
    return pl.pallas_call(
        update,
        name="adam_blend",
        out_shape=(
            jax.ShapeDtypeStruct((1, FEAT, COLS), BF16),
            jax.ShapeDtypeStruct((FEAT, COLS), F32),
        ),
        in_specs=[vmem] * 8,
        out_specs=(any_space, any_space),
        scratch_shapes=[pltpu.VMEM((FEAT, COLS), BF16), dma((2 * PARTS,)), dma],
        compiler_params=pltpu.CompilerParams(vmem_limit_bytes=16 * 2**20),
    )(*parts)


def solution(mesh):
    placed = (
        P("rep", "fsdp", None),
        P("rep", "fsdp", None),
        P("rep", "fsdp", None),
        P("fsdp", None),
        P("fsdp", None),
        P("rep", "fsdp", None),
        P("rep", "fsdp", None),
        P("fsdp"),
        P(),
        P("rep"),
    )
    return jax.shard_map(
        local,
        mesh=mesh,
        in_specs=placed,
        out_specs=(P("rep", "fsdp", None), P("fsdp", None)),
        check_vma=False,
    )
```
